32 devices in a mesh: bond: 4 (over y, core), atom: 8 (over z, x).
Axes of the slice: x: 2, y: 2, z: 4, core: 2. Of those that a mesh axis runs over, the one named last changes fastest.
Arguments:
- bond_states: bfloat16 [65536, 512], P(('bond', 'atom')), may hold values from -6 to 6
- block_counts: int32 [32], P(('bond', 'atom')), may hold values from 8 to 64, as said below
- send_rows: int32 [32, 32, 64], P(('bond', 'atom')), may hold values from 0 to 2047
- source_slots: int32 [32, 2048], P(('bond', 'atom')), may hold values from 0 to 2047
- target_slots: int32 [32, 2048], P(('bond', 'atom')), may hold values from 0 to 1023
- return_rows: int32 [32, 1024], P(('bond', 'atom')), may hold values from 0 to 2047
- angular_basis: bfloat16 [2048, 32, 512], P(('bond', 'atom')), may hold values from -1 to 1
- pre_inner: bfloat16 [2, 512, 512], replicated, may hold values from -0.25 to 0.25
- pre_outer: bfloat16 [2, 512, 512], replicated, may hold values from -0.25 to 0.25
- down_proj: bfloat16 [2, 512, 64], replicated, may hold values from -0.25 to 0.25
- bilinear: bfloat16 [2, 1024, 64], replicated, may hold values from -0.1875 to 0.1875
- up_proj: bfloat16 [2, 64, 512], replicated, may hold values from -0.75 to 0.75
- post_inner: bfloat16 [2, 512, 512], replicated, may hold values from -0.25 to 0.25
- post_outer: bfloat16 [2, 512, 512], replicated, may hold values from -0.25 to 0.25
Outputs:
- bond_out: bfloat16 [65536, 512], P(('bond', 'atom'))
The draws below stay inside these ranges and needn't reach their ends.
Inputs may be any that keep to these rules, and one draw needn't show every extreme that they name: Owner o's blocks numbered below block_counts[o] are live, the others are padding; some owner has all 64 live in every draw.
All inputs are finite; a program needn't handle non-finite values.
Results may differ from the reference program's by a relative error of at most 0.0078.
Values may be sent and summed in bfloat16 or wider, within the bound.
No kernel may reach another device: no remote copies, remote signals or barrier semaphores. Data moves between devices by JAX's collectives and lax.ppermute only.
A program may use at most 128 MiB of HBM per device.

```python
import jax
import jax.numpy as jnp
from jax import lax

D = 512
TRIP = 64
NSPH = 16
BLK = 32
LAYERS = 2
CAP = 64
CAP2 = 32
BOND_DEV = 2048
NB = 64
PEERS = 32
BONDS = 65536


def draw_block_counts(key, part):
    first_key = jax.random.fold_in(key, 11)
    second_key = jax.random.fold_in(key, 12)
    lowest = max(1, NB // 8)
    counts = jax.random.randint(first_key, (PEERS,), lowest, NB // 2 + 1, dtype=jnp.int32)
    busiest = jax.random.randint(second_key, (4,), 0, PEERS, dtype=jnp.int32)
    counts = counts.at[busiest].set(NB)
    return counts.astype(jnp.int32)


def plant(result, rng, low, largest):
    spot = [jax.random.randint(jax.random.fold_in(rng, axis), (), 0, length) for axis, length in enumerate(result.shape)]
    main_axis = result.shape.index(max(result.shape))
    beside = spot[:main_axis] + [(spot[main_axis] + 1) % result.shape[main_axis]] + spot[main_axis + 1:]
    return result.at[tuple(spot)].set(low).at[tuple(beside)].set(largest)


def shard_levels(rng, extent, cuts, low, top_value):
    def one(dim, blocks):
        heights = jax.random.uniform(jax.random.fold_in(jax.random.fold_in(rng, 6), dim), (blocks,), jnp.float32, low / len(cuts), top_value / len(cuts))
        return jnp.repeat(jnp.exp(heights), extent[dim] // blocks).reshape((-1,) + (1,) * (len(extent) - dim - 1))

    level = one(*cuts[0])
    for cut in cuts[1:]:
        level = level * one(*cut)
    return level


def normal_values(rng, extent, width, bound, cuts=(), held_as=jnp.bfloat16):
    gain = shard_levels(rng, extent, cuts, -0.22, 0.18) if cuts else 1.0
    array = jax.random.normal(rng, extent, jnp.float32) * width * gain
    return jnp.minimum(jnp.maximum(array, -bound), bound).astype(held_as)


def setup_inputs(seed: int = 0) -> dict:
    seeds = jax.random.split(jax.random.key(seed), 15)
    bond_states = normal_values(seeds[0], (BONDS, D), 1.0, 6.0, ((0, 32),))
    block_counts = draw_block_counts(jax.random.fold_in(seeds[14], 71), 0)
    send_rows = plant(jax.random.randint(seeds[2], (PEERS, PEERS, CAP), 0, BOND_DEV), jax.random.fold_in(seeds[2], 1), 0, BOND_DEV - 1).astype(jnp.int32)
    source_slots = plant(jax.random.randint(seeds[3], (PEERS, NB * BLK), 0, PEERS * CAP), jax.random.fold_in(seeds[3], 1), 0, (PEERS * CAP) - 1).astype(jnp.int32)
    target_slots = plant(jax.random.randint(seeds[4], (PEERS, NB * BLK), 0, PEERS * CAP2), jax.random.fold_in(seeds[4], 1), 0, (PEERS * CAP2) - 1).astype(jnp.int32)
    return_rows = plant(jax.random.randint(seeds[5], (PEERS, PEERS * CAP2), 0, BOND_DEV), jax.random.fold_in(seeds[5], 1), 0, BOND_DEV - 1).astype(jnp.int32)
    angular_basis = normal_values(seeds[6], (PEERS * NB, BLK, BLK * NSPH), BLK ** -0.5, 1.0, ((0, 32),))
    pre_inner = normal_values(seeds[7], (LAYERS, D, D), D ** -0.5, 0.25)
    pre_outer = normal_values(seeds[8], (LAYERS, D, D), D ** -0.5, 0.25)
    down_proj = normal_values(seeds[9], (LAYERS, D, TRIP), D ** -0.5, 0.25)
    bilinear = normal_values(seeds[10], (LAYERS, NSPH * TRIP, TRIP), (NSPH * TRIP) ** -0.5, 0.1875)
    up_proj = normal_values(seeds[11], (LAYERS, TRIP, D), TRIP ** -0.5, 0.75)
    post_inner = normal_values(seeds[12], (LAYERS, D, D), D ** -0.5, 0.25)
    post_outer = normal_values(seeds[13], (LAYERS, D, D), D ** -0.5, 0.25)
    return dict(bond_states=bond_states, block_counts=block_counts, send_rows=send_rows, source_slots=source_slots, target_slots=target_slots, return_rows=return_rows, angular_basis=angular_basis, pre_inner=pre_inner, pre_outer=pre_outer, down_proj=down_proj, bilinear=bilinear, up_proj=up_proj, post_inner=post_inner, post_outer=post_outer)


root_half = 0.7071067811865476


def residual(states, inner_weight, outer_weight):
    hidden = jax.nn.silu(jnp.dot(states, inner_weight, preferred_element_type=jnp.float32)).astype(jnp.bfloat16)
    return (states.astype(jnp.float32) + jax.nn.silu(jnp.dot(hidden, outer_weight, preferred_element_type=jnp.float32))) * root_half


def reference(bond_states, block_counts, send_rows, source_slots, target_slots, return_rows, angular_basis, pre_inner, pre_outer, down_proj, bilinear, up_proj, post_inner, post_outer):
    device_ids = jnp.arange(PEERS, dtype=jnp.int32)
    fetch_rows = (send_rows + device_ids[:, None, None] * BOND_DEV).astype(jnp.int32)
    fetch_rows = jnp.transpose(fetch_rows, (1, 0, 2)).reshape(PEERS, PEERS * CAP)
    block_basis = angular_basis.reshape(PEERS, NB, BLK, BLK * NSPH)
    live_blocks = (jnp.arange(NB, dtype=jnp.int32)[None, :] < block_counts[:, None]).astype(jnp.float32)
    return_ids = (return_rows + device_ids[:, None] * BOND_DEV).astype(jnp.int32).reshape(-1)
    states = bond_states
    for layer_index in range(LAYERS):
        inner_state = residual(states, pre_inner[layer_index], pre_outer[layer_index]).astype(jnp.bfloat16)
        projected = jax.nn.silu(jnp.dot(inner_state, down_proj[layer_index], preferred_element_type=jnp.float32)).astype(jnp.bfloat16)
        weight_bil = bilinear[layer_index]

        def owner_work(pieces):
            fetch_owner, source_owner, target_owner, basis_owner, live_owner = pieces
            provided = projected[fetch_owner]
            gathered = provided[source_owner].reshape(NB, BLK, TRIP)
            contracted = jnp.einsum("bsx,bsc->bxc", basis_owner.astype(jnp.float32), gathered.astype(jnp.float32)).astype(jnp.bfloat16)
            partial_rows = jnp.dot(contracted.reshape(NB * BLK, NSPH * TRIP), weight_bil, preferred_element_type=jnp.float32)
            partial_rows = partial_rows * jnp.repeat(live_owner, BLK)[:, None]
            slot_sums = jax.ops.segment_sum(partial_rows, target_owner, num_segments=PEERS * CAP2)
            return slot_sums.astype(jnp.bfloat16)

        slot_sums = lax.map(owner_work, (fetch_rows, source_slots, target_slots, block_basis, live_blocks))
        values = jnp.transpose(slot_sums.reshape(PEERS, PEERS, CAP2, TRIP), (1, 0, 2, 3)).reshape(-1, TRIP)
        message = jax.ops.segment_sum(values.astype(jnp.float32), return_ids, num_segments=BONDS).astype(jnp.bfloat16)
        joined = ((inner_state.astype(jnp.float32) + jax.nn.silu(jnp.dot(message, up_proj[layer_index], preferred_element_type=jnp.float32))) * root_half).astype(jnp.bfloat16)
        states = residual(joined, post_inner[layer_index], post_outer[layer_index]).astype(jnp.bfloat16)
    return states
```

```python
import functools

import jax
import jax.numpy as jnp
from jax import lax
from jax.experimental import pallas as pl
from jax.experimental.pallas import tpu as pltpu
from jax.sharding import PartitionSpec as P

root_half = 0.7071067811865476
LANES = 128
HIGH = 256
BLOCKS_IN_GROUP = 8
SLOT_ROWS = 8
VMEM_BYTES = 48 * 1024 * 1024

bf16 = jnp.bfloat16
f32 = jnp.float32
i32 = jnp.int32


def mm(a, b):
    return jnp.dot(a, b, preferred_element_type=f32)


def mm_nt(a, b):
    return lax.dot_general(a, b, (((1,), (1,)), ((), ())), preferred_element_type=f32)


def silu_of_half(u):
    return u + u * jnp.tanh(u)


def half_weight(ref):
    return ref[...] * bf16(0.5)


def lane(shape):
    return lax.broadcasted_iota(i32, shape, 1)


def one_hot_rows(high):
    at = lane(high.shape)
    parts = [jnp.where(high == at + k * LANES, f32(1), f32(0)).astype(bf16) for k in range(HIGH // LANES)]
    return jnp.concatenate(parts, axis=1)


def column(row):
    return jnp.transpose(jnp.broadcast_to(row, (LANES, LANES)))


def swap_halves(v):
    return pltpu.roll(v, v.shape[1] // 2, 1)


def pick_group(wide, group, count):
    picked = wide[:, :LANES]
    for m in range(1, count):
        picked = jnp.where(group == m, wide[:, m * LANES : (m + 1) * LANES], picked)
    return picked


def residual_rows(x, inner_half, outer_half):
    hidden = silu_of_half(mm(x, inner_half)).astype(bf16)
    return ((x.astype(f32) + silu_of_half(mm(hidden, outer_half))) * root_half).astype(bf16)


def project_pair(inner_rows, down_t):
    zero = jnp.zeros_like(down_t)
    left = jnp.concatenate([down_t, zero], axis=0)
    right = jnp.concatenate([zero, down_t], axis=0)
    u = mm_nt(inner_rows[:HIGH], left) + mm_nt(inner_rows[HIGH:], right)
    return silu_of_half(u).astype(bf16)


def write_payload(send_ref, table_ref, payload_ref):
    owners, cap = send_ref.shape
    half_cap = cap // 2
    pack = LANES // half_cap
    groups = table_ref.shape[1] // LANES
    table = table_ref[...]
    low_half = lane((LANES, LANES)) < LANES // 2
    for first in range(0, owners, pack):
        columns = [
            jnp.transpose(jnp.concatenate([jnp.broadcast_to(send_ref[o : o + 1, :], (LANES, cap))] * (LANES // cap), axis=1))
            for o in range(first, first + pack)
        ]
        sides = []
        for side in range(2):
            rows = jnp.concatenate([c[side * half_cap : (side + 1) * half_cap] for c in columns], axis=0)
            wide = mm(one_hot_rows(rows & (HIGH - 1)), table)
            low = rows >> 8
            picked = pick_group(wide, low >> 1, groups)
            sides.append(jnp.where((low & 1) == side, picked, swap_halves(picked)))
        packed = jnp.where(low_half, sides[0], sides[1]).astype(bf16)
        payload_ref[first * half_cap : (first + pack) * half_cap, :] = packed


def first_kernel(x_ref, send_ref, inner_ref, outer_ref, down_ref, out_ref, payload_ref, table_ref):
    step = pl.program_id(0)
    rows = residual_rows(x_ref[...], half_weight(inner_ref), half_weight(outer_ref))
    out_ref[...] = rows
    table_ref[:, pl.ds(pl.multiple_of(step * LANES, LANES), LANES)] = project_pair(rows, half_weight(down_ref))

    @pl.when(step == pl.num_programs(0) - 1)
    def _():
        write_payload(send_ref, table_ref, payload_ref)


def gather_messages(incoming_ref, return_pick_ref, return_low_ref, message_ref):
    slots = incoming_ref.shape[0]
    low_half = lane((slots, LANES)) < LANES // 2
    upper = jnp.where(low_half, 0, 1)
    groups = message_ref.shape[1] // LANES
    pieces = []
    for g in range(return_low_ref.shape[0]):
        m, side = divmod(g, 2)
        both = incoming_ref[:, m * LANES : (m + 1) * LANES].astype(f32)
        other = swap_halves(both)
        spread = jnp.where(low_half, both, other) if side == 0 else jnp.where(low_half, other, both)
        low = return_low_ref[g]
        pieces.append(
            jnp.concatenate(
                [jnp.where(low == 2 * k + upper, spread, f32(0)).astype(bf16) for k in range(groups)], axis=1
            )
        )
    message_ref[...] = mm(return_pick_ref[...], jnp.concatenate(pieces, axis=0)).astype(bf16)


def join_rows(inner, message, up_half):
    zero = jnp.zeros_like(up_half)
    u = jnp.concatenate(
        [
            mm(message, jnp.concatenate([up_half, zero], axis=0)),
            mm(message, jnp.concatenate([zero, up_half], axis=0)),
        ],
        axis=0,
    )
    return ((inner.astype(f32) + silu_of_half(u)) * root_half).astype(bf16)


def middle_kernel(
    incoming_ref,
    return_pick_ref,
    return_low_ref,
    x_ref,
    up_ref,
    post_inner_ref,
    post_outer_ref,
    send_ref,
    inner_ref,
    outer_ref,
    down_ref,
    out_ref,
    payload_ref,
    message_ref,
    table_ref,
):
    step = pl.program_id(0)

    @pl.when(step == 0)
    def _():
        gather_messages(incoming_ref, return_pick_ref, return_low_ref, message_ref)

    at = pl.ds(pl.multiple_of(step * LANES, LANES), LANES)
    joined = join_rows(x_ref[...], message_ref[:, at], half_weight(up_ref))
    state = residual_rows(joined, half_weight(post_inner_ref), half_weight(post_outer_ref))
    rows = residual_rows(state, half_weight(inner_ref), half_weight(outer_ref))
    out_ref[...] = rows
    table_ref[:, at] = project_pair(rows, half_weight(down_ref))

    @pl.when(step == pl.num_programs(0) - 1)
    def _():
        write_payload(send_ref, table_ref, payload_ref)


def last_kernel(
    incoming_ref, return_pick_ref, return_low_ref, x_ref, up_ref, post_inner_ref, post_outer_ref, out_ref, message_ref
):
    step = pl.program_id(0)

    @pl.when(step == 0)
    def _():
        gather_messages(incoming_ref, return_pick_ref, return_low_ref, message_ref)

    at = pl.ds(pl.multiple_of(step * LANES, LANES), LANES)
    joined = join_rows(x_ref[...], message_ref[:, at], half_weight(up_ref))
    out_ref[...] = residual_rows(joined, half_weight(post_inner_ref), half_weight(post_outer_ref))


def prepare_kernel(
    cap,
    cap_back,
    counts_ref,
    source_ref,
    target_ref,
    return_ref,
    basis_ref,
    bilinear_ref,
    basis_out,
    weight_out,
    source_pick_out,
    source_code_out,
    target_pick_out,
    target_low_out,
    return_pick_out,
    return_low_out,
):
    blocks, width, span = basis_ref.shape
    sph = span // width
    layers, trip, _ = bilinear_ref.shape
    groups = blocks // BLOCKS_IN_GROUP
    chunks = source_ref.shape[1] // LANES
    side_blocks = LANES // width
    half_cap = cap // 2
    to = lax.broadcasted_iota(i32, (span, span), 0)
    order = jnp.where(lane((span, span)) == (to % width) * sph + to // width, f32(1), f32(0)).astype(bf16)
    for g in range(groups):
        rows = jnp.concatenate(
            [
                basis_ref[g * side_blocks : (g + 1) * side_blocks].reshape(LANES, span),
                basis_ref[blocks // 2 + g * side_blocks : blocks // 2 + (g + 1) * side_blocks].reshape(LANES, span),
            ],
            axis=0,
        )
        basis_out[g] = mm_nt(order, rows).astype(bf16)
    zero = jnp.zeros((trip, LANES), bf16)
    for layer in range(layers):
        for k in range(0, sph, 2):
            pair = jnp.transpose(bilinear_ref[layer, :, k * trip : (k + 2) * trip].astype(f32))
            both = jnp.concatenate([pair, pair], axis=1).astype(bf16)
            for j in range(2):
                w = both[j * trip : (j + 1) * trip]
                base = (k + j) * 2 * trip
                weight_out[layer, base : base + trip, :] = jnp.concatenate([w, zero], axis=1)
                weight_out[layer, base + trip : base + 2 * trip, :] = jnp.concatenate([zero, w], axis=1)
    for chunk in range(chunks):
        side, g = divmod(chunk, groups)
        s = column(source_ref[:, chunk * LANES : (chunk + 1) * LANES])
        rho = (s // cap) * half_cap + s % half_cap
        half = (s // half_cap) % 2
        rows = slice(side * LANES, (side + 1) * LANES)
        source_pick_out[g, rows, :] = one_hot_rows(rho & (HIGH - 1))
        source_code_out[g, rows, :] = (rho >> 8) * 2 + (half ^ side)
    count = counts_ref[0]
    highs = target_pick_out.shape[0]
    for chunk in range(chunks):
        cols = slice(chunk * LANES, (chunk + 1) * LANES)
        row = target_ref[:, cols]
        target_low_out[cols, :] = (column(row) % cap_back) // SLOT_ROWS
        high = (row // cap_back) * SLOT_ROWS + row % SLOT_ROWS
        live = (lane(row.shape) + chunk * LANES) // width < count
        high = jnp.broadcast_to(jnp.where(live, high, -1), (LANES, LANES))
        for h in range(highs // LANES):
            at = lax.broadcasted_iota(i32, (LANES, LANES), 0) + h * LANES
            target_pick_out[h * LANES : (h + 1) * LANES, cols] = jnp.where(high == at, f32(1), f32(0)).astype(bf16)
    parts = cap_back // SLOT_ROWS
    owners_in = LANES // cap_back
    for chunk in range(return_ref.shape[1] // LANES):
        col = column(return_ref[:, chunk * LANES : (chunk + 1) * LANES])
        for o in range(owners_in):
            for g in range(parts):
                base = (chunk * owners_in + o) * SLOT_ROWS
                return_low_out[g, base : base + SLOT_ROWS, :] = col[(o * parts + g) * SLOT_ROWS : (o * parts + g + 1) * SLOT_ROWS]
    slots = return_low_out.shape[1]
    for g in range(parts):
        for chunk in range(slots // LANES):
            rows = slice(chunk * LANES, (chunk + 1) * LANES)
            r = return_low_out[g, rows, :]
            high = jnp.transpose(r) & (HIGH - 1)
            return_low_out[g, rows, :] = r >> 8
            for h in range(HIGH // LANES):
                at = lax.broadcasted_iota(i32, (LANES, LANES), 0) + h * LANES
                cols = slice(g * slots + chunk * LANES, g * slots + (chunk + 1) * LANES)
                return_pick_out[h * LANES : (h + 1) * LANES, cols] = jnp.where(high == at, f32(1), f32(0)).astype(bf16)


def owner_kernel(
    arrived_ref,
    source_pick_ref,
    source_code_ref,
    basis_ref,
    weight_ref,
    target_low_ref,
    target_pick_ref,
    out_ref,
    spread_ref,
):
    step = pl.program_id(0)
    span = basis_ref.shape[0]
    width = LANES // (BLOCKS_IN_GROUP // 2)
    sph = span // width
    tables = arrived_ref.shape[0] // HIGH
    table = jnp.concatenate([arrived_ref[m * HIGH : (m + 1) * HIGH, :] for m in range(tables)], axis=1)
    wide = mm(source_pick_ref[...], table)
    code = source_code_ref[...]
    picked = pick_group(wide, code >> 1, tables)
    turned = jnp.where((code & 1) == 1, swap_halves(picked), picked)
    row = lax.broadcasted_iota(i32, turned.shape, 0)
    upper_lane = lane(turned.shape) >= LANES // 2
    kept = jnp.where((row >= LANES) == upper_lane, turned, f32(0)).astype(bf16)
    columns = []
    for j in range(BLOCKS_IN_GROUP // 2):
        pieces = []
        for side in range(2):
            for k in range(BLOCKS_IN_GROUP // 2):
                base = side * LANES + k * width
                pieces.append(kept[base : base + width] if k == j else jnp.zeros((width, LANES), bf16))
        columns.append(jnp.concatenate(pieces, axis=0))
    contracted = mm(basis_ref[...], jnp.concatenate(columns, axis=1)).astype(bf16)
    lhs = jnp.concatenate(
        [
            jnp.concatenate(
                [contracted[k * width : (k + 1) * width, j * LANES : (j + 1) * LANES] for k in range(sph)], axis=1
            )
            for j in range(BLOCKS_IN_GROUP // 2)
        ],
        axis=0,
    )
    partial = mm(lhs, weight_ref[...])
    upper = jnp.where(lane((LANES, LANES)) < LANES // 2, 0, 1)
    groups = spread_ref.shape[1] // LANES
    half_rows = spread_ref.shape[0] // 2
    for side in range(2):
        rows = pl.ds(pl.multiple_of(side * half_rows + step * LANES, LANES), LANES)
        low = target_low_ref[rows, :]
        values = partial[:, side * LANES : (side + 1) * LANES]
        for m in range(groups):
            spread_ref[rows, m * LANES : (m + 1) * LANES] = jnp.where(low == 2 * m + upper, values, f32(0)).astype(bf16)

    @pl.when(step == pl.num_programs(0) - 1)
    def _():
        out_ref[...] = mm(target_pick_ref[...], spread_ref[...]).astype(bf16)


def whole(shape):
    return pl.BlockSpec(shape, lambda *_: (0,) * len(shape))


def of_layer(shape, layer):
    return pl.BlockSpec((None,) + shape[1:], lambda *_: (layer,) + (0,) * (len(shape) - 1))


def params():
    return pltpu.CompilerParams(vmem_limit_bytes=VMEM_BYTES, dimension_semantics=("arbitrary",))


def on_device(
    bond_states,
    block_counts,
    send_rows,
    source_slots,
    target_slots,
    return_rows,
    angular_basis,
    pre_inner,
    pre_outer,
    down_proj,
    bilinear,
    up_proj,
    post_inner,
    post_outer,
):
    axes = ("bond", "atom")
    peers = lax.axis_size("bond") * lax.axis_size("atom")
    rows, depth = bond_states.shape
    blocks, width, span = angular_basis.shape
    layers, _, trip = down_proj.shape
    cap = send_rows.shape[2]
    returns = return_rows.shape[1]
    cap_back = returns // peers
    pair = 2 * HIGH
    steps = rows // pair
    lookup = peers * cap // 2
    slots = peers * SLOT_ROWS
    slot_lanes = cap_back // SLOT_ROWS * trip
    groups = blocks // BLOCKS_IN_GROUP
    group_rows = BLOCKS_IN_GROUP * width
    send = send_rows.reshape(peers, cap)
    down_t = jnp.swapaxes(down_proj, 1, 2)
    bilinear_t = jnp.swapaxes(bilinear, 1, 2)
    row_block = pl.BlockSpec((pair, depth), lambda i: (i, 0))
    row_shape = jax.ShapeDtypeStruct((rows, depth), bf16)
    payload_shape = jax.ShapeDtypeStruct((lookup, LANES), bf16)
    table_scratch = pltpu.VMEM((HIGH, rows // HIGH * trip), bf16)

    def exchange(values, per_peer):
        values = values.reshape(peers, per_peer, values.shape[1])
        got = lax.all_to_all(values, axes, split_axis=0, concat_axis=0, tiled=True)
        return got.reshape(peers * per_peer, values.shape[2])

    inner, payload = pl.pallas_call(
        first_kernel,
        grid=(steps,),
        in_specs=[
            row_block,
            whole(send.shape),
            of_layer(pre_inner.shape, 0),
            of_layer(pre_outer.shape, 0),
            of_layer(down_t.shape, 0),
        ],
        out_specs=[row_block, whole(payload_shape.shape)],
        out_shape=[row_shape, payload_shape],
        scratch_shapes=[table_scratch],
        compiler_params=params(),
        name="first",
    )(bond_states, send, pre_inner, pre_outer, down_t)

    prepared_shapes = [
        jax.ShapeDtypeStruct((groups, span, group_rows), bf16),
        jax.ShapeDtypeStruct((layers, bilinear.shape[1] * 2, 2 * LANES), bf16),
        jax.ShapeDtypeStruct((groups, group_rows, HIGH), bf16),
        jax.ShapeDtypeStruct((groups, group_rows, LANES), i32),
        jax.ShapeDtypeStruct((slots, blocks * width), bf16),
        jax.ShapeDtypeStruct((blocks * width, LANES), i32),
        jax.ShapeDtypeStruct((HIGH, returns), bf16),
        jax.ShapeDtypeStruct((cap_back // SLOT_ROWS, slots, LANES), i32),
    ]
    prepared = pl.pallas_call(
        functools.partial(prepare_kernel, cap, cap_back),
        in_specs=[pl.BlockSpec(memory_space=pltpu.SMEM)] + [pl.BlockSpec(memory_space=pltpu.VMEM)] * 5,
        out_specs=[pl.BlockSpec(memory_space=pltpu.VMEM)] * len(prepared_shapes),
        out_shape=prepared_shapes,
        compiler_params=pltpu.CompilerParams(vmem_limit_bytes=VMEM_BYTES),
        cost_estimate=pl.CostEstimate(flops=4 * 10**9, bytes_accessed=12 * 10**6, transcendentals=0),
        name="prepare",
    )(block_counts, source_slots, target_slots, return_rows, angular_basis, bilinear_t)
    basis, weight, source_pick, source_code, target_pick, target_low, return_pick, return_low = prepared

    out = None
    for layer in range(layers):
        arrived = exchange(payload, cap // 2)
        slot_sums = pl.pallas_call(
            owner_kernel,
            grid=(groups,),
            in_specs=[
                whole(arrived.shape),
                pl.BlockSpec((None, group_rows, HIGH), lambda i: (i, 0, 0)),
                pl.BlockSpec((None, group_rows, LANES), lambda i: (i, 0, 0)),
                pl.BlockSpec((None, span, group_rows), lambda i: (i, 0, 0)),
                of_layer(weight.shape, layer),
                whole(target_low.shape),
                whole(target_pick.shape),
            ],
            out_specs=whole((slots, slot_lanes)),
            out_shape=jax.ShapeDtypeStruct((slots, slot_lanes), bf16),
            scratch_shapes=[pltpu.VMEM((blocks * width, slot_lanes), bf16)],
            compiler_params=params(),
            name="owner",
        )(arrived, source_pick, source_code, basis, weight, target_low, target_pick)
        incoming = exchange(slot_sums, SLOT_ROWS)
        head = [incoming, return_pick, return_low, inner, up_proj, post_inner, post_outer]
        head_specs = [
            whole(incoming.shape),
            whole(return_pick.shape),
            whole(return_low.shape),
            row_block,
            of_layer(up_proj.shape, layer),
            of_layer(post_inner.shape, layer),
            of_layer(post_outer.shape, layer),
        ]
        message_scratch = pltpu.VMEM((HIGH, rows // HIGH * trip), bf16)
        if layer + 1 < layers:
            inner, payload = pl.pallas_call(
                middle_kernel,
                grid=(steps,),
                in_specs=head_specs
                + [
                    whole(send.shape),
                    of_layer(pre_inner.shape, layer + 1),
                    of_layer(pre_outer.shape, layer + 1),
                    of_layer(down_t.shape, layer + 1),
                ],
                out_specs=[row_block, whole(payload_shape.shape)],
                out_shape=[row_shape, payload_shape],
                scratch_shapes=[message_scratch, table_scratch],
                compiler_params=params(),
                name="middle",
            )(*head, send, pre_inner, pre_outer, down_t)
        else:
            out = pl.pallas_call(
                last_kernel,
                grid=(steps,),
                in_specs=head_specs,
                out_specs=row_block,
                out_shape=row_shape,
                scratch_shapes=[message_scratch],
                compiler_params=params(),
                name="last",
            )(*head)
    return out


def solution(mesh):
    split = ("bond", "atom")
    in_specs = (
        P(split, None),
        P(split),
        P(split, None, None),
        P(split, None),
        P(split, None),
        P(split, None),
        P(split, None, None),
    ) + (P(),) * 7
    return jax.shard_map(on_device, mesh=mesh, in_specs=in_specs, out_specs=P(split, None), check_vma=False)
```

```python
import functools

import jax
import jax.numpy as jnp
from jax import lax
from jax.experimental import pallas as pl
from jax.experimental.pallas import tpu as pltpu
from jax.sharding import PartitionSpec as P

root_half = 0.7071067811865476
LANES = 128
HIGH = 256
PAIR = 512
BLOCKS_IN_GROUP = 8
SLOT_ROWS = 8
MIB = 1024 * 1024

bf16 = jnp.bfloat16
f32 = jnp.float32
i32 = jnp.int32


def mm(a, b):
    return jnp.dot(a, b, preferred_element_type=f32)


def mm_nt(a, b):
    return lax.dot_general(a, b, (((1,), (1,)), ((), ())), preferred_element_type=f32)


def silu_of_half(u):
    return u + u * jnp.tanh(u)


def half_weight(ref):
    return ref[...] * bf16(0.5)


def lane(shape):
    return lax.broadcasted_iota(i32, shape, 1)


def one_hot_rows(high):
    at = lane(high.shape).astype(f32)
    parts = [jnp.where(high == at + k * LANES, f32(1), f32(0)).astype(bf16) for k in range(HIGH // LANES)]
    return jnp.concatenate(parts, axis=1)


def on_diagonal(values):
    row = lax.broadcasted_iota(i32, values.shape, 0)
    return jnp.where(row == lane(values.shape), values, f32(0)).astype(bf16)


def columns_of(rows):
    ones = jnp.ones((LANES, LANES), bf16)
    stacked = jnp.concatenate([on_diagonal(jnp.broadcast_to(r.astype(f32), (LANES, LANES))) for r in rows], axis=0)
    wide = mm(stacked, ones)
    return [wide[k * LANES : (k + 1) * LANES] for k in range(len(rows))]


def rows_of(column):
    return mm(jnp.ones((LANES, LANES), bf16), on_diagonal(column))


def swap_halves(v):
    return pltpu.roll(v, v.shape[1] // 2, 1)


def pick_group(wide, group, count):
    picked = wide[:, :LANES]
    for m in range(1, count):
        picked = jnp.where(group == m, wide[:, m * LANES : (m + 1) * LANES], picked)
    return picked


def residual_rows(x, inner_half, outer_half):
    hidden = silu_of_half(mm(x, inner_half)).astype(bf16)
    return ((x.astype(f32) + silu_of_half(mm(hidden, outer_half))) * root_half).astype(bf16)


def project_pair(inner_rows, down_t):
    zero = jnp.zeros_like(down_t)
    left = jnp.concatenate([down_t, zero], axis=0)
    right = jnp.concatenate([zero, down_t], axis=0)
    u = mm_nt(inner_rows[:HIGH], left) + mm_nt(inner_rows[HIGH:], right)
    return silu_of_half(u).astype(bf16)


def pick_sends(send_ref, pick_ref, low_ref, first, last):
    cap = send_ref.shape[1]
    half_cap = cap // 2
    pack = LANES // half_cap
    for base in range(first, last, pack):
        highs = []
        lows = []
        for o in range(base, base + pack, LANES // cap):
            row = jnp.concatenate([send_ref[o + k : o + k + 1, :] for k in range(LANES // cap)], axis=1)
            high, low = columns_of([row & (HIGH - 1), row >> 8])
            highs.append(high)
            lows.append(low)
        high = jnp.concatenate(highs, axis=0)
        low = jnp.concatenate(lows, axis=0)
        rows = slice(base * half_cap, (base + pack) * half_cap)
        for side in range(2):
            at = [slice(k * cap + side * half_cap, k * cap + (side + 1) * half_cap) for k in range(pack)]
            pick_ref[side, rows, :] = one_hot_rows(jnp.concatenate([high[t] for t in at], axis=0))
            low_ref[side, rows, :] = jnp.concatenate([low[t] for t in at], axis=0).astype(i32)


def write_payload(pick_ref, low_ref, table_ref, payload_ref):
    groups = table_ref.shape[1] // LANES
    table = table_ref[...]
    low_half = lane((HIGH, LANES)) < LANES // 2
    for base in range(0, payload_ref.shape[0], HIGH):
        sides = []
        for side in range(2):
            wide = mm(pick_ref[side, base : base + HIGH, :], table)
            low = low_ref[side, base : base + HIGH, :]
            picked = pick_group(wide, low >> 1, groups)
            sides.append(jnp.where((low & 1) == side, picked, swap_halves(picked)))
        payload_ref[base : base + HIGH, :] = jnp.where(low_half, sides[0], sides[1]).astype(bf16)


class Fetch:
    def __init__(self, sems, pairs):
        self.copies = [pltpu.make_async_copy(src, dst, sems.at[k]) for k, (src, dst) in enumerate(pairs)]
        for copy in self.copies:
            copy.start()

    def wait(self, *which):
        for k in which or range(len(self.copies)):
            self.copies[k].wait()


def row_chunks(ref):
    return [slice(base, base + PAIR) for base in range(0, ref.shape[0], PAIR)]


def first_kernel(
    layer,
    x_hbm,
    send_hbm,
    inner_hbm,
    outer_hbm,
    down_hbm,
    out_hbm,
    payload_ref,
    x_ref,
    send_ref,
    inner_ref,
    outer_ref,
    down_ref,
    out_ref,
    table_ref,
    pick_ref,
    low_ref,
    sems,
    out_sems,
):
    rows_half = x_ref.shape[0] // 2
    fetch = Fetch(
        sems,
        [
            (send_hbm, send_ref),
            (inner_hbm.at[layer], inner_ref),
            (outer_hbm.at[layer], outer_ref),
            (down_hbm.at[layer], down_ref),
            (x_hbm.at[0:rows_half], x_ref.at[0:rows_half]),
            (x_hbm.at[rows_half : 2 * rows_half], x_ref.at[rows_half : 2 * rows_half]),
        ],
    )
    fetch.wait(0)
    pick_sends(send_ref, pick_ref, low_ref, 0, send_ref.shape[0])
    fetch.wait(1, 2, 3, 4)
    inner_half, outer_half, down_half = half_weight(inner_ref), half_weight(outer_ref), half_weight(down_ref)
    for k, c in enumerate(row_chunks(x_ref)):
        if c.start == rows_half:
            fetch.wait(5)
        rows = residual_rows(x_ref[c, :], inner_half, outer_half)
        out_ref[c, :] = rows
        table_ref[:, k * LANES : (k + 1) * LANES] = project_pair(rows, down_half)
    store = Fetch(out_sems, [(out_ref, out_hbm)])
    write_payload(pick_ref, low_ref, table_ref, payload_ref)
    store.wait()


def gather_messages(incoming_ref, return_pick_ref, return_low_ref, message_ref):
    slots = incoming_ref.shape[0]
    low_half = lane((slots, LANES)) < LANES // 2
    upper = jnp.where(low_half, 0, 1)
    groups = message_ref.shape[1] // LANES
    pieces = []
    for g in range(return_low_ref.shape[0]):
        m, side = divmod(g, 2)
        both = incoming_ref[:, m * LANES : (m + 1) * LANES].astype(f32)
        other = swap_halves(both)
        spread = jnp.where(low_half, both, other) if side == 0 else jnp.where(low_half, other, both)
        low = return_low_ref[g]
        pieces.append(
            jnp.concatenate(
                [jnp.where(low == 2 * k + upper, spread, f32(0)).astype(bf16) for k in range(groups)], axis=1
            )
        )
    message_ref[...] = mm(return_pick_ref[...], jnp.concatenate(pieces, axis=0)).astype(bf16)


def join_rows(inner, message, up_half):
    zero = jnp.zeros_like(up_half)
    u = jnp.concatenate(
        [
            mm(message, jnp.concatenate([up_half, zero], axis=0)),
            mm(message, jnp.concatenate([zero, up_half], axis=0)),
        ],
        axis=0,
    )
    return ((inner.astype(f32) + silu_of_half(u)) * root_half).astype(bf16)


def middle_kernel(
    layer,
    incoming_ref,
    return_pick_ref,
    return_low_ref,
    x_ref,
    up_ref,
    post_inner_ref,
    post_outer_ref,
    pick_ref,
    low_ref,
    inner_ref,
    outer_ref,
    down_ref,
    out_ref,
    payload_ref,
    message_ref,
    table_ref,
):
    gather_messages(incoming_ref, return_pick_ref, return_low_ref, message_ref)
    up_half = half_weight(up_ref.at[layer])
    post_inner_half, post_outer_half = half_weight(post_inner_ref.at[layer]), half_weight(post_outer_ref.at[layer])
    inner_half, outer_half = half_weight(inner_ref.at[layer + 1]), half_weight(outer_ref.at[layer + 1])
    down_half = half_weight(down_ref.at[layer + 1])
    for k, c in enumerate(row_chunks(x_ref)):
        joined = join_rows(x_ref[c, :], message_ref[:, k * LANES : (k + 1) * LANES], up_half)
        state = residual_rows(joined, post_inner_half, post_outer_half)
        rows = residual_rows(state, inner_half, outer_half)
        out_ref[c, :] = rows
        table_ref[:, k * LANES : (k + 1) * LANES] = project_pair(rows, down_half)
    write_payload(pick_ref, low_ref, table_ref, payload_ref)


def last_kernel(
    layer,
    incoming_ref,
    return_pick_ref,
    return_low_ref,
    x_ref,
    up_ref,
    post_inner_ref,
    post_outer_ref,
    out_hbm,
    out_ref,
    message_ref,
    out_sems,
):
    gather_messages(incoming_ref, return_pick_ref, return_low_ref, message_ref)
    up_half = half_weight(up_ref.at[layer])
    post_inner_half, post_outer_half = half_weight(post_inner_ref.at[layer]), half_weight(post_outer_ref.at[layer])
    chunks = row_chunks(x_ref)
    stores = []
    for half in range(2):
        part = range(half * len(chunks) // 2, (half + 1) * len(chunks) // 2)
        for k in part:
            c = chunks[k]
            joined = join_rows(x_ref[c, :], message_ref[:, k * LANES : (k + 1) * LANES], up_half)
            out_ref[c, :] = residual_rows(joined, post_inner_half, post_outer_half)
        rows = slice(part[0] * PAIR, (part[-1] + 1) * PAIR)
        store = pltpu.make_async_copy(out_ref.at[rows], out_hbm.at[rows], out_sems.at[half])
        store.start()
        stores.append(store)
    for store in stores:
        store.wait()


def prepare_kernel(
    cap,
    cap_back,
    counts_ref,
    source_ref,
    target_ref,
    return_ref,
    send_ref,
    basis_hbm,
    bilinear_hbm,
    basis_out,
    source_out,
    weight_hbm,
    target_pick_hbm,
    target_low_hbm,
    return_pick_hbm,
    return_low_hbm,
    send_pick_hbm,
    send_low_hbm,
    basis_ref,
    bilinear_ref,
    weight_out,
    target_pick_out,
    target_low_out,
    return_pick_out,
    return_low_out,
    send_pick_out,
    send_low_out,
    high_ref,
    sems,
    out_sems,
):
    fetch = Fetch(sems, [(basis_hbm, basis_ref), (bilinear_hbm, bilinear_ref)])
    prepare_returns(cap_back, return_ref, return_pick_out, return_low_out, high_ref)
    pick_sends(send_ref, send_pick_out, send_low_out, 0, send_ref.shape[0])
    prepare_slots(cap, cap_back, counts_ref, source_ref, target_ref, source_out, target_pick_out, target_low_out, basis_ref.shape)
    fetch.wait()
    spread_weight(bilinear_ref, weight_out)
    stores = Fetch(
        out_sems,
        [
            (weight_out, weight_hbm),
            (target_pick_out, target_pick_hbm),
            (target_low_out, target_low_hbm),
            (return_pick_out, return_pick_hbm),
            (return_low_out, return_low_hbm),
            (send_pick_out, send_pick_hbm),
            (send_low_out, send_low_hbm),
        ],
    )
    turn_basis(basis_ref, basis_out)
    stores.wait()


def turn_basis(basis_ref, basis_out):
    blocks, width, span = basis_ref.shape
    sph = span // width
    groups = blocks // BLOCKS_IN_GROUP
    side_blocks = LANES // width
    to = lax.broadcasted_iota(i32, (span, span), 0)
    order = jnp.where(lane((span, span)) == (to % width) * sph + to // width, f32(1), f32(0)).astype(bf16)
    for g in range(groups):
        rows = jnp.concatenate(
            [
                basis_ref[g * side_blocks : (g + 1) * side_blocks].reshape(LANES, span),
                basis_ref[blocks // 2 + g * side_blocks : blocks // 2 + (g + 1) * side_blocks].reshape(LANES, span),
            ],
            axis=0,
        )
        basis_out[g] = mm_nt(order, rows).astype(bf16)


def spread_weight(bilinear_ref, weight_out):
    layers, trip, depth = bilinear_ref.shape
    zero = jnp.zeros((trip, LANES), bf16)
    for layer in range(layers):
        for k in range(0, depth // trip, 2):
            pair = jnp.transpose(bilinear_ref[layer, :, k * trip : (k + 2) * trip].astype(f32))
            both = jnp.concatenate([pair, pair], axis=1).astype(bf16)
            for j in range(2):
                w = both[j * trip : (j + 1) * trip]
                base = (k + j) * 2 * trip
                weight_out[layer, base : base + trip, :] = jnp.concatenate([w, zero], axis=1)
                weight_out[layer, base + trip : base + 2 * trip, :] = jnp.concatenate([zero, w], axis=1)


def prepare_slots(cap, cap_back, counts_ref, source_ref, target_ref, source_out, target_pick_out, target_low_out, basis_shape):
    blocks, width, _ = basis_shape
    groups = blocks // BLOCKS_IN_GROUP
    chunks = source_ref.shape[1] // LANES
    half_cap = cap // 2
    for chunk in range(chunks):
        side, g = divmod(chunk, groups)
        cols = slice(chunk * LANES, (chunk + 1) * LANES)
        s = source_ref[:, cols]
        rho = (s // cap) * half_cap + s % half_cap
        half = (s // half_cap) % 2
        row = target_ref[:, cols]
        picks, codes, lows = columns_of(
            [rho & (HIGH - 1), (rho >> 8) * 2 + (half ^ side), (row % cap_back) // SLOT_ROWS]
        )
        rows = slice(side * LANES, (side + 1) * LANES)
        source_out[g, rows, :] = (picks + codes * HIGH).astype(i32)
        target_low_out[cols, :] = lows.astype(i32)
    count = counts_ref[0]
    highs = target_pick_out.shape[0]
    for chunk in range(chunks):
        cols = slice(chunk * LANES, (chunk + 1) * LANES)
        row = target_ref[:, cols]
        high = (row // cap_back) * SLOT_ROWS + row % SLOT_ROWS
        live = (lane(row.shape) + chunk * LANES) // width < count
        high = jnp.broadcast_to(jnp.where(live, high, -1), (LANES, LANES))
        for h in range(highs // LANES):
            at = lax.broadcasted_iota(i32, (LANES, LANES), 0) + h * LANES
            target_pick_out[h * LANES : (h + 1) * LANES, cols] = jnp.where(high == at, f32(1), f32(0)).astype(bf16)


def prepare_returns(cap_back, return_ref, return_pick_out, return_low_out, high_ref):
    parts = cap_back // SLOT_ROWS
    owners_in = LANES // cap_back
    for chunk in range(return_ref.shape[1] // LANES):
        row = return_ref[:, chunk * LANES : (chunk + 1) * LANES]
        high, low = columns_of([row & (HIGH - 1), row >> 8])
        low = low.astype(i32)
        for o in range(owners_in):
            for g in range(parts):
                to = slice((chunk * owners_in + o) * SLOT_ROWS, (chunk * owners_in + o + 1) * SLOT_ROWS)
                at = slice((o * parts + g) * SLOT_ROWS, (o * parts + g + 1) * SLOT_ROWS)
                return_low_out[g, to, :] = low[at]
                high_ref[g, to, :] = high[at]
    slots = return_low_out.shape[1]
    for g in range(parts):
        for chunk in range(slots // LANES):
            high = rows_of(high_ref[g, chunk * LANES : (chunk + 1) * LANES, :])
            cols = slice(g * slots + chunk * LANES, g * slots + (chunk + 1) * LANES)
            for h in range(HIGH // LANES):
                at = (lax.broadcasted_iota(i32, (LANES, LANES), 0) + h * LANES).astype(f32)
                return_pick_out[h * LANES : (h + 1) * LANES, cols] = jnp.where(high == at, f32(1), f32(0)).astype(bf16)


def block_diagonal(kept, width):
    half_blocks = BLOCKS_IN_GROUP // 2
    zero = jnp.zeros((width, LANES), bf16)
    columns = []
    for j in range(half_blocks):
        pieces = []
        for side in range(2):
            for k in range(half_blocks):
                base = side * LANES + k * width
                pieces.append(kept[base : base + width] if k == j else zero)
        columns.append(jnp.concatenate(pieces, axis=0))
    return jnp.concatenate(columns, axis=1)


def owner_kernel(
    layer,
    arrived_ref,
    source_ref,
    basis_ref,
    weight_hbm,
    target_low_hbm,
    target_pick_hbm,
    out_ref,
    weight_ref,
    target_low_ref,
    target_pick_ref,
    kept_ref,
    lhs_ref,
    spread_ref,
    sems,
):
    fetch = Fetch(
        sems, [(weight_hbm.at[layer], weight_ref), (target_low_hbm, target_low_ref), (target_pick_hbm, target_pick_ref)]
    )
    groups, span, group_rows = basis_ref.shape
    half_blocks = BLOCKS_IN_GROUP // 2
    width = LANES // half_blocks
    sph = span // width
    tables = arrived_ref.shape[0] // HIGH
    table = jnp.concatenate([arrived_ref[m * HIGH : (m + 1) * HIGH, :] for m in range(tables)], axis=1)
    shape = (group_rows, LANES)
    own_half = (lax.broadcasted_iota(i32, shape, 0) >= LANES) == (lane(shape) >= LANES // 2)
    for g in range(groups):
        source = source_ref[g]
        wide = mm(one_hot_rows((source & (HIGH - 1)).astype(f32)), table)
        code = source >> 8
        picked = pick_group(wide, code >> 1, tables)
        turned = jnp.where((code & 1) == 1, swap_halves(picked), picked)
        kept_ref[g] = jnp.where(own_half, turned, f32(0)).astype(bf16)
    for g in range(groups):
        contracted = mm(basis_ref[g], block_diagonal(kept_ref[g], width)).astype(bf16)
        for j in range(half_blocks):
            rows = slice(g * LANES + j * width, g * LANES + (j + 1) * width)
            for k in range(sph):
                lhs_ref[rows, k * LANES : (k + 1) * LANES] = contracted[k * width : (k + 1) * width, j * LANES : (j + 1) * LANES]
    fetch.wait()
    half_rows = lhs_ref.shape[0]
    chunk = min(half_rows, PAIR)
    upper = jnp.where(lane((chunk, LANES)) < LANES // 2, 0, 1)
    lane_groups = spread_ref.shape[1] // LANES
    for base in range(0, half_rows, chunk):
        partial = mm(lhs_ref[base : base + chunk, :], weight_ref[...])
        for side in range(2):
            rows = slice(side * half_rows + base, side * half_rows + base + chunk)
            low = target_low_ref[rows, :]
            values = partial[:, side * LANES : (side + 1) * LANES]
            for m in range(lane_groups):
                spread_ref[rows, m * LANES : (m + 1) * LANES] = jnp.where(low == 2 * m + upper, values, f32(0)).astype(bf16)
    out_ref[...] = mm(target_pick_ref[...], spread_ref[...]).astype(bf16)


IN_HBM = pl.BlockSpec(memory_space=pl.ANY)
IN_VMEM = pl.BlockSpec(memory_space=pltpu.VMEM)
IN_SMEM = pl.BlockSpec(memory_space=pltpu.SMEM)


def run(kernel, name, in_specs, outs, scratch, operands, mib=32, flops=10**9):
    out_specs, out_shapes = zip(*outs)
    return pl.pallas_call(
        kernel,
        in_specs=in_specs,
        out_specs=list(out_specs),
        out_shape=list(out_shapes),
        scratch_shapes=scratch,
        compiler_params=pltpu.CompilerParams(vmem_limit_bytes=mib * MIB),
        cost_estimate=pl.CostEstimate(flops=flops, bytes_accessed=8 * 10**6, transcendentals=0),
        name=name,
    )(*operands)


def like(array):
    return pltpu.VMEM(array.shape, array.dtype)


def of_layer(array):
    return pltpu.VMEM(array.shape[1:], array.dtype)


def on_device(
    bond_states,
    block_counts,
    send_rows,
    source_slots,
    target_slots,
    return_rows,
    angular_basis,
    pre_inner,
    pre_outer,
    down_proj,
    bilinear,
    up_proj,
    post_inner,
    post_outer,
):
    axes = ("bond", "atom")
    peers = lax.axis_size("bond") * lax.axis_size("atom")
    rows, depth = bond_states.shape
    blocks, width, span = angular_basis.shape
    layers, _, trip = down_proj.shape
    cap = send_rows.shape[2]
    returns = return_rows.shape[1]
    cap_back = returns // peers
    lookup = peers * cap // 2
    slots = peers * SLOT_ROWS
    slot_lanes = cap_back // SLOT_ROWS * trip
    groups = blocks // BLOCKS_IN_GROUP
    group_rows = BLOCKS_IN_GROUP * width
    send = send_rows.reshape(peers, cap)
    down_t = jnp.swapaxes(down_proj, 1, 2)
    bilinear_t = jnp.swapaxes(bilinear, 1, 2)
    shape_of = jax.ShapeDtypeStruct
    row_shape = shape_of((rows, depth), bf16)
    payload_shape = shape_of((lookup, LANES), bf16)
    pick_shape = (2, lookup, HIGH)
    low_shape = (2, lookup, LANES)
    wide_scratch = pltpu.VMEM((HIGH, rows // HIGH * trip), bf16)
    row_scratch = pltpu.VMEM((rows, depth), bf16)

    def exchange(values, per_peer):
        values = values.reshape(peers, per_peer, values.shape[1])
        got = lax.all_to_all(values, axes, split_axis=0, concat_axis=0, tiled=True)
        return got.reshape(peers * per_peer, values.shape[2])

    inner, payload = run(
        functools.partial(first_kernel, 0),
        "first",
        [IN_HBM] * 5,
        [(IN_HBM, row_shape), (IN_VMEM, payload_shape)],
        [row_scratch, like(send), of_layer(pre_inner), of_layer(pre_outer), of_layer(down_t), row_scratch, wide_scratch]
        + [pltpu.VMEM(pick_shape, bf16), pltpu.VMEM(low_shape, i32)]
        + [pltpu.SemaphoreType.DMA((6,)), pltpu.SemaphoreType.DMA((1,))],
        (bond_states, send, pre_inner, pre_outer, down_t),
        mib=60,
    )

    kept_shapes = [shape_of((groups, span, group_rows), bf16), shape_of((groups, group_rows, LANES), i32)]
    stored_shapes = [
        shape_of((layers, bilinear.shape[1] * 2, 2 * LANES), bf16),
        shape_of((slots, blocks * width), bf16),
        shape_of((blocks * width, LANES), i32),
        shape_of((HIGH, returns), bf16),
        shape_of((cap_back // SLOT_ROWS, slots, LANES), i32),
        shape_of(pick_shape, bf16),
        shape_of(low_shape, i32),
    ]
    basis, source, weight, target_pick, target_low, return_pick, return_low, send_pick, send_low = run(
        functools.partial(prepare_kernel, cap, cap_back),
        "prepare",
        [IN_SMEM] + [IN_VMEM] * 4 + [IN_HBM] * 2,
        [(IN_VMEM, shape) for shape in kept_shapes] + [(IN_HBM, shape) for shape in stored_shapes],
        [like(angular_basis), like(bilinear_t)]
        + [like(shape) for shape in stored_shapes]
        + [pltpu.VMEM((cap_back // SLOT_ROWS, slots, LANES), f32)]
        + [pltpu.SemaphoreType.DMA((2,)), pltpu.SemaphoreType.DMA((len(stored_shapes),))],
        (block_counts, source_slots, target_slots, return_rows, send, angular_basis, bilinear_t),
        mib=48,
        flops=4 * 10**9,
    )

    out = None
    for layer in range(layers):
        arrived = exchange(payload, cap // 2)
        (slot_sums,) = run(
            functools.partial(owner_kernel, layer),
            "owner",
            [IN_VMEM] * 3 + [IN_HBM] * 3,
            [(IN_VMEM, shape_of((slots, slot_lanes), bf16))],
            [of_layer(weight), like(target_low), like(target_pick)]
            + [pltpu.VMEM((groups, group_rows, LANES), bf16)]
            + [pltpu.VMEM((blocks * width // 2, weight.shape[1]), bf16), pltpu.VMEM((blocks * width, slot_lanes), bf16)]
            + [pltpu.SemaphoreType.DMA((3,))],
            (arrived, source, basis, weight, target_low, target_pick),
        )
        incoming = exchange(slot_sums, SLOT_ROWS)
        head = (incoming, return_pick, return_low, inner, up_proj, post_inner, post_outer)
        if layer + 1 < layers:
            inner, payload = run(
                functools.partial(middle_kernel, layer),
                "middle",
                [IN_VMEM] * 12,
                [(IN_VMEM, row_shape), (IN_VMEM, payload_shape)],
                [wide_scratch, wide_scratch],
                head + (send_pick, send_low, pre_inner, pre_outer, down_t),
            )
        else:
            (out,) = run(
                functools.partial(last_kernel, layer),
                "last",
                [IN_VMEM] * 7,
                [(IN_HBM, row_shape)],
                [row_scratch, wide_scratch, pltpu.SemaphoreType.DMA((2,))],
                head,
            )
    return out


def solution(mesh):
    split = ("bond", "atom")
    in_specs = (
        P(split, None),
        P(split),
        P(split, None, None),
        P(split, None),
        P(split, None),
        P(split, None),
        P(split, None, None),
    ) + (P(),) * 7
    return jax.shard_map(on_device, mesh=mesh, in_specs=in_specs, out_specs=P(split, None), check_vma=False)
```

```python
import functools

import jax
import jax.numpy as jnp
from jax import lax
from jax.experimental import pallas as pl
from jax.experimental.pallas import tpu as pltpu
from jax.sharding import PartitionSpec as P

root_half = 0.7071067811865476
LANES = 128
HIGH = 256
PAIR = 512
BLOCKS_IN_GROUP = 8
SLOT_ROWS = 8
MIB = 1024 * 1024

bf16 = jnp.bfloat16
f32 = jnp.float32
i32 = jnp.int32


def mm(a, b):
    return jnp.dot(a, b, preferred_element_type=f32)


def mm_nt(a, b):
    return lax.dot_general(a, b, (((1,), (1,)), ((), ())), preferred_element_type=f32)


def silu_of_half(u):
    return u + u * jnp.tanh(u)


def half_weight(ref):
    return ref[...] * bf16(0.5)


def lane(shape):
    return lax.broadcasted_iota(i32, shape, 1)


def one_hot_rows(high):
    at = lane(high.shape).astype(f32)
    parts = [jnp.where(high == at + k * LANES, f32(1), f32(0)).astype(bf16) for k in range(HIGH // LANES)]
    return jnp.concatenate(parts, axis=1)


def on_diagonal(values):
    row = lax.broadcasted_iota(i32, values.shape, 0)
    return jnp.where(row == lane(values.shape), values, f32(0)).astype(bf16)


def columns_of(rows):
    ones = jnp.ones((LANES, LANES), bf16)
    stacked = jnp.concatenate([on_diagonal(jnp.broadcast_to(r.astype(f32), (LANES, LANES))) for r in rows], axis=0)
    wide = mm(stacked, ones)
    return [wide[k * LANES : (k + 1) * LANES] for k in range(len(rows))]


def rows_of(column):
    return mm(jnp.ones((LANES, LANES), bf16), on_diagonal(column))


def swap_halves(v):
    return pltpu.roll(v, v.shape[1] // 2, 1)


def pick_group(wide, group, count):
    picked = wide[:, :LANES]
    for m in range(1, count):
        picked = jnp.where(group == m, wide[:, m * LANES : (m + 1) * LANES], picked)
    return picked


def residual_rows(x, inner_half, outer_half):
    hidden = silu_of_half(mm(x, inner_half)).astype(bf16)
    return ((x.astype(f32) + silu_of_half(mm(hidden, outer_half))) * root_half).astype(bf16)


def project_pair(inner_rows, down_t):
    zero = jnp.zeros_like(down_t)
    left = jnp.concatenate([down_t, zero], axis=0)
    right = jnp.concatenate([zero, down_t], axis=0)
    u = mm_nt(inner_rows[:HIGH], left) + mm_nt(inner_rows[HIGH:], right)
    return silu_of_half(u).astype(bf16)


def pack_sends(send_ref, packed_ref):
    owners, cap = send_ref.shape
    half_cap = cap // 2
    pack = LANES // half_cap
    for base in range(0, owners, pack):
        packed = []
        for o in range(base, base + pack, LANES // cap):
            row = jnp.concatenate([send_ref[o + k : o + k + 1, :] for k in range(LANES // cap)], axis=1)
            high, low = columns_of([row & (HIGH - 1), row >> 8])
            packed.append((high + low * HIGH).astype(i32))
        packed = jnp.concatenate(packed, axis=0)
        rows = slice(base * half_cap, (base + pack) * half_cap)
        for side in range(2):
            at = [slice(k * cap + side * half_cap, k * cap + (side + 1) * half_cap) for k in range(pack)]
            packed_ref[side, rows, :] = jnp.concatenate([packed[t] for t in at], axis=0)


def write_payload(packed_ref, table_ref, payload_ref):
    groups = table_ref.shape[1] // LANES
    table = table_ref[...]
    low_half = lane((HIGH, LANES)) < LANES // 2
    for base in range(0, payload_ref.shape[0], HIGH):
        sides = []
        for side in range(2):
            packed = packed_ref[side, base : base + HIGH, :]
            wide = mm(one_hot_rows((packed & (HIGH - 1)).astype(f32)), table)
            low = packed >> 8
            picked = pick_group(wide, low >> 1, groups)
            sides.append(jnp.where((low & 1) == side, picked, swap_halves(picked)))
        payload_ref[base : base + HIGH, :] = jnp.where(low_half, sides[0], sides[1]).astype(bf16)


class Fetch:
    def __init__(self, sems, pairs):
        self.copies = [pltpu.make_async_copy(src, dst, sems.at[k]) for k, (src, dst) in enumerate(pairs)]
        for copy in self.copies:
            copy.start()

    def wait(self, *which):
        for k in which or range(len(self.copies)):
            self.copies[k].wait()


def row_chunks(ref):
    return [slice(base, base + PAIR) for base in range(0, ref.shape[0], PAIR)]


def first_kernel(
    layers,
    x_hbm,
    send_hbm,
    inner_hbm,
    outer_hbm,
    down_hbm,
    post_inner_hbm,
    post_outer_hbm,
    out_hbm,
    payload_ref,
    *rest,
):
    layer = 0
    split = [(w, n) for w in (post_inner_hbm, post_outer_hbm) for n in range(layers)]
    split += [(w, n) for w in (inner_hbm, outer_hbm) for n in range(1, layers)]
    split_out = rest[: len(split)]
    (
        x_ref,
        send_ref,
        inner_ref,
        outer_ref,
        down_ref,
        out_ref,
        table_ref,
        packed_ref,
        split_ref,
        sems,
        out_sems,
        load_sems,
        split_sems,
    ) = rest[len(split) :]
    rows_half = x_ref.shape[0] // 2
    fetch = Fetch(
        sems,
        [
            (send_hbm, send_ref),
            (inner_hbm.at[layer], inner_ref),
            (outer_hbm.at[layer], outer_ref),
            (down_hbm.at[layer], down_ref),
            (x_hbm.at[0:rows_half], x_ref.at[0:rows_half]),
            (x_hbm.at[rows_half : 2 * rows_half], x_ref.at[rows_half : 2 * rows_half]),
        ],
    )
    fetch.wait(0)
    pack_sends(send_ref, packed_ref)
    fetch.wait(1, 2, 3, 4)
    loads = Fetch(load_sems, [(w.at[n], split_ref.at[k]) for k, (w, n) in enumerate(split)])
    inner_half, outer_half, down_half = half_weight(inner_ref), half_weight(outer_ref), half_weight(down_ref)
    halves = [slice(0, rows_half), slice(rows_half, 2 * rows_half)]
    stores = [pltpu.make_async_copy(out_ref.at[h], out_hbm.at[h], out_sems.at[k]) for k, h in enumerate(halves)]
    for k, c in enumerate(row_chunks(x_ref)):
        if c.start == rows_half:
            stores[0].start()
            fetch.wait(5)
            loads.wait()
            copies = Fetch(split_sems, [(split_ref.at[n], to) for n, to in enumerate(split_out)])
        rows = residual_rows(x_ref[c, :], inner_half, outer_half)
        out_ref[c, :] = rows
        table_ref[:, k * LANES : (k + 1) * LANES] = project_pair(rows, down_half)
    stores[1].start()
    write_payload(packed_ref, table_ref, payload_ref)
    for store in stores:
        store.wait()
    copies.wait()


def one_hot_columns(high_ref, slab, first, count, n):
    rows = [high_ref[slab, first + k : first + k + 1, :] for k in range(n // LANES)]
    high = jnp.concatenate(rows, axis=1).astype(f32)
    at = lax.broadcasted_iota(i32, (count, high.shape[1]), 0).astype(f32)
    return jnp.where(high == at, f32(1), f32(0)).astype(bf16)


def gather_messages(incoming_ref, return_low_ref, message_ref):
    slots = incoming_ref.shape[0]
    low_half = lane((slots, LANES)) < LANES // 2
    upper = jnp.where(low_half, 0, 1)
    groups = message_ref.shape[1] // LANES
    total = None
    parts = return_low_ref.shape[0] - 1
    for g in range(parts):
        m, side = divmod(g, 2)
        both = incoming_ref[:, m * LANES : (m + 1) * LANES].astype(f32)
        other = swap_halves(both)
        spread = jnp.where(low_half, both, other) if side == 0 else jnp.where(low_half, other, both)
        low = return_low_ref[g]
        piece = jnp.concatenate(
            [jnp.where(low == 2 * k + upper, spread, f32(0)).astype(bf16) for k in range(groups)], axis=1
        )
        part = mm(one_hot_columns(return_low_ref, parts, g * (slots // LANES), HIGH, slots), piece)
        total = part if total is None else total + part
    message_ref[...] = total.astype(bf16)


def join_rows(inner, message, up_half):
    zero = jnp.zeros_like(up_half)
    u = jnp.concatenate(
        [
            mm(message, jnp.concatenate([up_half, zero], axis=0)),
            mm(message, jnp.concatenate([zero, up_half], axis=0)),
        ],
        axis=0,
    )
    return ((inner.astype(f32) + silu_of_half(u)) * root_half).astype(bf16)


def middle_kernel(
    layer,
    incoming_ref,
    return_low_ref,
    x_hbm,
    up_ref,
    post_inner_ref,
    post_outer_ref,
    send_ref,
    down_ref,
    inner_ref,
    outer_ref,
    out_hbm,
    payload_ref,
    x_ref,
    out_ref,
    message_ref,
    table_ref,
    packed_ref,
    sems,
    out_sems,
):
    rows_half = x_ref.shape[0] // 2
    halves = [slice(0, rows_half), slice(rows_half, 2 * rows_half)]
    fetch = Fetch(sems, [(x_hbm.at[h], x_ref.at[h]) for h in halves])
    stores = [pltpu.make_async_copy(out_ref.at[h], out_hbm.at[h], out_sems.at[k]) for k, h in enumerate(halves)]
    gather_messages(incoming_ref, return_low_ref, message_ref)
    up_half = half_weight(up_ref.at[layer])
    post_inner_half, post_outer_half = half_weight(post_inner_ref), half_weight(post_outer_ref)
    inner_half, outer_half = half_weight(inner_ref), half_weight(outer_ref)
    down_half = half_weight(down_ref.at[layer + 1])
    fetch.wait(0)
    for k, c in enumerate(row_chunks(x_ref)):
        if c.start == rows_half:
            stores[0].start()
            fetch.wait(1)
        joined = join_rows(x_ref[c, :], message_ref[:, k * LANES : (k + 1) * LANES], up_half)
        state = residual_rows(joined, post_inner_half, post_outer_half)
        rows = residual_rows(state, inner_half, outer_half)
        out_ref[c, :] = rows
        table_ref[:, k * LANES : (k + 1) * LANES] = project_pair(rows, down_half)
    stores[1].start()
    pack_sends(send_ref, packed_ref)
    write_payload(packed_ref, table_ref, payload_ref)
    for store in stores:
        store.wait()


def last_kernel(
    layer,
    incoming_ref,
    return_low_ref,
    x_ref,
    up_ref,
    post_inner_ref,
    post_outer_ref,
    out_hbm,
    out_ref,
    message_ref,
    out_sems,
):
    gather_messages(incoming_ref, return_low_ref, message_ref)
    up_half = half_weight(up_ref.at[layer])
    post_inner_half, post_outer_half = half_weight(post_inner_ref), half_weight(post_outer_ref)
    chunks = row_chunks(x_ref)
    stores = []
    count = len(chunks)
    bounds = [0, count // 2, count - 1, count]
    for n in range(3):
        part = range(bounds[n], bounds[n + 1])
        for k in part:
            c = chunks[k]
            joined = join_rows(x_ref[c, :], message_ref[:, k * LANES : (k + 1) * LANES], up_half)
            out_ref[c, :] = residual_rows(joined, post_inner_half, post_outer_half)
        rows = slice(part[0] * PAIR, (part[-1] + 1) * PAIR)
        store = pltpu.make_async_copy(out_ref.at[rows], out_hbm.at[rows], out_sems.at[n])
        store.start()
        stores.append(store)
    for store in stores:
        store.wait()


def prepare_kernel(
    cap,
    cap_back,
    counts_ref,
    source_ref,
    target_ref,
    return_ref,
    basis_hbm,
    bilinear_hbm,
    basis_out,
    source_out,
    return_low_out,
    basis_ref,
    bilinear_ref,
    high_ref,
    sems,
):
    fetch = Fetch(sems, [(basis_hbm, basis_ref), (bilinear_hbm, bilinear_ref)])
    prepare_returns(cap_back, return_ref, return_low_out, high_ref)
    prepare_slots(cap, cap_back, counts_ref, source_ref, target_ref, source_out, basis_ref.shape)
    fetch.wait()
    turn_basis(basis_ref, basis_out)
    layers, trip, depth = bilinear_ref.shape
    width = basis_out.shape[2]
    slab = basis_out.shape[0] - 1
    for layer in range(layers):
        for piece in range(depth // width):
            base = (layer * (depth // width) + piece) * trip
            basis_out[slab, base : base + trip, :] = bilinear_ref[layer, :, piece * width : (piece + 1) * width]


def turn_basis(basis_ref, basis_out):
    blocks, width, span = basis_ref.shape
    sph = span // width
    groups = blocks // BLOCKS_IN_GROUP
    side_blocks = LANES // width
    to = lax.broadcasted_iota(i32, (span, span), 0)
    order = jnp.where(lane((span, span)) == (to % width) * sph + to // width, f32(1), f32(0)).astype(bf16)
    for g in range(groups):
        rows = jnp.concatenate(
            [
                basis_ref[g * side_blocks : (g + 1) * side_blocks].reshape(LANES, span),
                basis_ref[blocks // 2 + g * side_blocks : blocks // 2 + (g + 1) * side_blocks].reshape(LANES, span),
            ],
            axis=0,
        )
        basis_out[g] = mm_nt(order, rows).astype(bf16)


def spread_weight(basis_ref, layer, trip, weight_out):
    slab, _, width = basis_ref.shape
    slab -= 1
    depth = weight_out.shape[0] // 2
    zero = jnp.zeros((trip, LANES), bf16)
    for k in range(0, depth // trip, 2):
        piece, at = divmod(k * trip, width)
        base = (layer * (depth // width) + piece) * trip
        pair = jnp.transpose(basis_ref[slab, base : base + trip, at : at + LANES].astype(f32))
        both = jnp.concatenate([pair, pair], axis=1).astype(bf16)
        for j in range(2):
            w = both[j * trip : (j + 1) * trip]
            base = (k + j) * 2 * trip
            weight_out[base : base + trip, :] = jnp.concatenate([w, zero], axis=1)
            weight_out[base + trip : base + 2 * trip, :] = jnp.concatenate([zero, w], axis=1)


def prepare_slots(cap, cap_back, counts_ref, source_ref, target_ref, source_out, basis_shape):
    blocks, width, _ = basis_shape
    groups = blocks // BLOCKS_IN_GROUP
    chunks = source_ref.shape[1] // LANES
    half_cap = cap // 2
    for chunk in range(chunks):
        side, g = divmod(chunk, groups)
        cols = slice(chunk * LANES, (chunk + 1) * LANES)
        s = source_ref[:, cols]
        rho = (s // cap) * half_cap + s % half_cap
        half = (s // half_cap) % 2
        row = target_ref[:, cols]
        picks, codes, lows = columns_of(
            [rho & (HIGH - 1), (rho >> 8) * 2 + (half ^ side), (row % cap_back) // SLOT_ROWS]
        )
        rows = slice(side * LANES, (side + 1) * LANES)
        source_out[g, rows, :] = (picks + codes * HIGH).astype(i32) + lows.astype(i32) * (HIGH * HIGH)
        live = (lane(row.shape) + chunk * LANES) // width < counts_ref[0]
        high = jnp.where(live, (row // cap_back) * SLOT_ROWS + row % SLOT_ROWS, -1)
        source_out[groups, chunk : chunk + 1, :] = high


def prepare_returns(cap_back, return_ref, return_low_out, high_ref):
    parts = cap_back // SLOT_ROWS
    owners_in = LANES // cap_back
    for chunk in range(return_ref.shape[1] // LANES):
        row = return_ref[:, chunk * LANES : (chunk + 1) * LANES]
        high, low = columns_of([row & (HIGH - 1), row >> 8])
        low = low.astype(i32)
        for o in range(owners_in):
            for g in range(parts):
                to = slice((chunk * owners_in + o) * SLOT_ROWS, (chunk * owners_in + o + 1) * SLOT_ROWS)
                at = slice((o * parts + g) * SLOT_ROWS, (o * parts + g + 1) * SLOT_ROWS)
                return_low_out[g, to, :] = low[at]
                high_ref[g, to, :] = high[at]
    slots = return_low_out.shape[1]
    for g in range(parts):
        for chunk in range(slots // LANES):
            high = rows_of(high_ref[g, chunk * LANES : (chunk + 1) * LANES, :])
            at = g * (slots // LANES) + chunk
            return_low_out[parts, at : at + 1, :] = high[0:1, :].astype(i32)


def block_diagonal(kept, width):
    half_blocks = BLOCKS_IN_GROUP // 2
    zero = jnp.zeros((width, LANES), bf16)
    columns = []
    for j in range(half_blocks):
        pieces = []
        for side in range(2):
            for k in range(half_blocks):
                base = side * LANES + k * width
                pieces.append(kept[base : base + width] if k == j else zero)
        columns.append(jnp.concatenate(pieces, axis=0))
    return jnp.concatenate(columns, axis=1)


def owner_kernel(
    layer,
    arrived_ref,
    source_ref,
    basis_ref,
    out_ref,
    weight_ref,
    kept_ref,
    lhs_ref,
    spread_ref,
):
    slabs, span, group_rows = basis_ref.shape
    groups = slabs - 1
    spread_weight(basis_ref, layer, LANES // 2, weight_ref)
    half_blocks = BLOCKS_IN_GROUP // 2
    width = LANES // half_blocks
    sph = span // width
    tables = arrived_ref.shape[0] // HIGH
    table = jnp.concatenate([arrived_ref[m * HIGH : (m + 1) * HIGH, :] for m in range(tables)], axis=1)
    shape = (group_rows, LANES)
    own_half = (lax.broadcasted_iota(i32, shape, 0) >= LANES) == (lane(shape) >= LANES // 2)
    for g in range(groups):
        source = source_ref[g]
        wide = mm(one_hot_rows((source & (HIGH - 1)).astype(f32)), table)
        code = (source >> 8) & (HIGH - 1)
        picked = pick_group(wide, code >> 1, tables)
        turned = jnp.where((code & 1) == 1, swap_halves(picked), picked)
        kept_ref[g] = jnp.where(own_half, turned, f32(0)).astype(bf16)
    for g in range(groups):
        contracted = mm(basis_ref[g], block_diagonal(kept_ref[g], width)).astype(bf16)
        for j in range(half_blocks):
            rows = slice(g * LANES + j * width, g * LANES + (j + 1) * width)
            for k in range(sph):
                lhs_ref[rows, k * LANES : (k + 1) * LANES] = contracted[k * width : (k + 1) * width, j * LANES : (j + 1) * LANES]
    half_rows = lhs_ref.shape[0]
    chunk = min(half_rows, PAIR)
    upper = jnp.where(lane((chunk, LANES)) < LANES // 2, 0, 1)
    lane_groups = spread_ref.shape[1] // LANES
    for base in range(0, half_rows, chunk):
        partial = mm(lhs_ref[base : base + chunk, :], weight_ref[...])
        for side in range(2):
            rows = slice(side * half_rows + base, side * half_rows + base + chunk)
            at = slice(side * LANES, (side + 1) * LANES)
            first = base // LANES
            low = jnp.concatenate([source_ref[g, at, :] >> 16 for g in range(first, first + chunk // LANES)], axis=0)
            values = partial[:, at]
            for m in range(lane_groups):
                spread_ref[rows, m * LANES : (m + 1) * LANES] = jnp.where(low == 2 * m + upper, values, f32(0)).astype(bf16)
    total = None
    for base in range(0, spread_ref.shape[0], chunk):
        part = mm(one_hot_columns(source_ref, groups, base // LANES, out_ref.shape[0], chunk), spread_ref[base : base + chunk, :])
        total = part if total is None else total + part
    out_ref[...] = total.astype(bf16)


IN_HBM = pl.BlockSpec(memory_space=pl.ANY)
IN_VMEM = pl.BlockSpec(memory_space=pltpu.VMEM)
IN_SMEM = pl.BlockSpec(memory_space=pltpu.SMEM)


def run(kernel, name, in_specs, outs, scratch, operands, mib=32, flops=10**9):
    out_specs, out_shapes = zip(*outs)
    return pl.pallas_call(
        kernel,
        in_specs=in_specs,
        out_specs=list(out_specs),
        out_shape=list(out_shapes),
        scratch_shapes=scratch,
        compiler_params=pltpu.CompilerParams(vmem_limit_bytes=mib * MIB),
        cost_estimate=pl.CostEstimate(flops=flops, bytes_accessed=8 * 10**6, transcendentals=0),
        name=name,
    )(*operands)


def like(array):
    return pltpu.VMEM(array.shape, array.dtype)


def of_layer(array):
    return pltpu.VMEM(array.shape[1:], array.dtype)


def on_device(
    bond_states,
    block_counts,
    send_rows,
    source_slots,
    target_slots,
    return_rows,
    angular_basis,
    pre_inner,
    pre_outer,
    down_proj,
    bilinear,
    up_proj,
    post_inner,
    post_outer,
):
    axes = ("bond", "atom")
    peers = lax.axis_size("bond") * lax.axis_size("atom")
    rows, depth = bond_states.shape
    blocks, width, span = angular_basis.shape
    layers, _, trip = down_proj.shape
    cap = send_rows.shape[2]
    returns = return_rows.shape[1]
    cap_back = returns // peers
    lookup = peers * cap // 2
    slots = peers * SLOT_ROWS
    slot_lanes = cap_back // SLOT_ROWS * trip
    groups = blocks // BLOCKS_IN_GROUP
    group_rows = BLOCKS_IN_GROUP * width
    send = send_rows.reshape(peers, cap)
    down_t = jnp.swapaxes(down_proj, 1, 2)
    bilinear_t = jnp.swapaxes(bilinear, 1, 2)
    shape_of = jax.ShapeDtypeStruct
    row_shape = shape_of((rows, depth), bf16)
    payload_shape = shape_of((lookup, LANES), bf16)
    packed_scratch = pltpu.VMEM((2, lookup, LANES), i32)
    wide_scratch = pltpu.VMEM((HIGH, rows // HIGH * trip), bf16)
    row_scratch = pltpu.VMEM((rows, depth), bf16)

    def exchange(values, per_peer):
        values = values.reshape(peers, per_peer, values.shape[1])
        got = lax.all_to_all(values, axes, split_axis=0, concat_axis=0, tiled=True)
        return got.reshape(peers * per_peer, values.shape[2])

    weight_shape = shape_of((depth, depth), bf16)
    splits = 2 * layers + 2 * (layers - 1)
    inner, payload, *weights = run(
        functools.partial(first_kernel, layers),
        "first",
        [IN_HBM] * 7,
        [(IN_HBM, row_shape), (IN_VMEM, payload_shape)] + [(IN_HBM, weight_shape)] * splits,
        [row_scratch, like(send), of_layer(pre_inner), of_layer(pre_outer), of_layer(down_t), row_scratch, wide_scratch]
        + [packed_scratch, pltpu.VMEM((splits, depth, depth), bf16)]
        + [pltpu.SemaphoreType.DMA((n,)) for n in (6, 2, splits, splits)],
        (bond_states, send, pre_inner, pre_outer, down_t, post_inner, post_outer),
        mib=60,
    )
    post_inners, post_outers = weights[:layers], weights[layers : 2 * layers]
    pre_inners = [None] + weights[2 * layers : 3 * layers - 1]
    pre_outers = [None] + weights[3 * layers - 1 :]

    parts = cap_back // SLOT_ROWS
    basis, source, return_low = run(
        functools.partial(prepare_kernel, cap, cap_back),
        "prepare",
        [IN_SMEM] + [IN_VMEM] * 3 + [IN_HBM] * 2,
        [
            (IN_VMEM, shape_of((groups + 1, span, group_rows), bf16)),
            (IN_VMEM, shape_of((groups + 1, group_rows, LANES), i32)),
            (IN_VMEM, shape_of((parts + 1, slots, LANES), i32)),
        ],
        [like(angular_basis), like(bilinear_t), pltpu.VMEM((parts, slots, LANES), f32), pltpu.SemaphoreType.DMA((2,))],
        (block_counts, source_slots, target_slots, return_rows, angular_basis, bilinear_t),
        flops=4 * 10**9,
    )

    out = None
    for layer in range(layers):
        arrived = exchange(payload, cap // 2)
        (slot_sums,) = run(
            functools.partial(owner_kernel, layer),
            "owner",
            [IN_VMEM] * 3,
            [(IN_VMEM, shape_of((slots, slot_lanes), bf16))],
            [
                pltpu.VMEM((bilinear.shape[1] * 2, 2 * LANES), bf16),
                pltpu.VMEM((groups, group_rows, LANES), bf16),
                pltpu.VMEM((blocks * width // 2, bilinear.shape[1] * 2), bf16),
                pltpu.VMEM((blocks * width, slot_lanes), bf16),
            ],
            (arrived, source, basis),
        )
        incoming = exchange(slot_sums, SLOT_ROWS)
        head = (incoming, return_low, inner, up_proj, post_inners[layer], post_outers[layer])
        if layer + 1 < layers:
            inner, payload = run(
                functools.partial(middle_kernel, layer),
                "middle",
                [IN_VMEM] * 2 + [IN_HBM] + [IN_VMEM] * 7,
                [(IN_HBM, row_shape), (IN_VMEM, payload_shape)],
                [row_scratch, row_scratch, wide_scratch, wide_scratch, packed_scratch]
                + [pltpu.SemaphoreType.DMA((2,)), pltpu.SemaphoreType.DMA((2,))],
                head + (send, down_t, pre_inners[layer + 1], pre_outers[layer + 1]),
                mib=49,
            )
        else:
            (out,) = run(
                functools.partial(last_kernel, layer),
                "last",
                [IN_VMEM] * 6,
                [(IN_HBM, row_shape)],
                [row_scratch, wide_scratch, pltpu.SemaphoreType.DMA((3,))],
                head,
            )
    return out


def solution(mesh):
    split = ("bond", "atom")
    in_specs = (
        P(split, None),
        P(split),
        P(split, None, None),
        P(split, None),
        P(split, None),
        P(split, None),
        P(split, None, None),
    ) + (P(),) * 7
    return jax.shard_map(on_device, mesh=mesh, in_specs=in_specs, out_specs=P(split, None), check_vma=False)
```

```python
import functools

import jax
import jax.numpy as jnp
from jax import lax
from jax.experimental import pallas as pl
from jax.experimental.pallas import tpu as pltpu
from jax.sharding import PartitionSpec as P

root_half = 0.7071067811865476
LANES = 128
HIGH = 256
PAIR = 512
BLOCKS_IN_GROUP = 8
SLOT_ROWS = 8
MIB = 1024 * 1024

bf16 = jnp.bfloat16
f32 = jnp.float32
i32 = jnp.int32


def mm(a, b):
    return jnp.dot(a, b, preferred_element_type=f32)


def mm_nt(a, b):
    return lax.dot_general(a, b, (((1,), (1,)), ((), ())), preferred_element_type=f32)


def silu_of_half(u):
    return u + u * jnp.tanh(u)


def half_weight(ref):
    return ref[...] * bf16(0.5)


def lane(shape):
    return lax.broadcasted_iota(i32, shape, 1)


def one_hot_rows(high):
    at = lane(high.shape).astype(f32)
    parts = [jnp.where(high == at + k * LANES, f32(1), f32(0)).astype(bf16) for k in range(HIGH // LANES)]
    return jnp.concatenate(parts, axis=1)


def on_diagonal(values):
    row = lax.broadcasted_iota(i32, values.shape, 0)
    return jnp.where(row == lane(values.shape), values, f32(0)).astype(bf16)


def columns_of(rows):
    ones = jnp.ones((LANES, LANES), bf16)
    stacked = jnp.concatenate([on_diagonal(jnp.broadcast_to(r.astype(f32), (LANES, LANES))) for r in rows], axis=0)
    wide = mm(stacked, ones)
    return [wide[k * LANES : (k + 1) * LANES] for k in range(len(rows))]


def rows_of(column):
    return mm(jnp.ones((LANES, LANES), bf16), on_diagonal(column))


def swap_halves(v):
    return pltpu.roll(v, v.shape[1] // 2, 1)


def pick_group(wide, group, count):
    picked = wide[:, :LANES]
    for m in range(1, count):
        picked = jnp.where(group == m, wide[:, m * LANES : (m + 1) * LANES], picked)
    return picked


def residual_rows(x, inner_half, outer_half):
    hidden = silu_of_half(mm(x, inner_half)).astype(bf16)
    return ((x.astype(f32) + silu_of_half(mm(hidden, outer_half))) * root_half).astype(bf16)


def project_pair(inner_rows, down_t):
    zero = jnp.zeros_like(down_t)
    left = jnp.concatenate([down_t, zero], axis=0)
    right = jnp.concatenate([zero, down_t], axis=0)
    u = mm_nt(inner_rows[:HIGH], left) + mm_nt(inner_rows[HIGH:], right)
    return silu_of_half(u).astype(bf16)


def pack_sends(send_ref, packed_ref):
    owners, cap = send_ref.shape
    half_cap = cap // 2
    pack = LANES // half_cap
    for base in range(0, owners, pack):
        packed = []
        for o in range(base, base + pack, LANES // cap):
            row = jnp.concatenate([send_ref[o + k : o + k + 1, :] for k in range(LANES // cap)], axis=1)
            high, low = columns_of([row & (HIGH - 1), row >> 8])
            packed.append((high + low * HIGH).astype(i32))
        packed = jnp.concatenate(packed, axis=0)
        rows = slice(base * half_cap, (base + pack) * half_cap)
        for side in range(2):
            at = [slice(k * cap + side * half_cap, k * cap + (side + 1) * half_cap) for k in range(pack)]
            packed_ref[side, rows, :] = jnp.concatenate([packed[t] for t in at], axis=0)


def write_payload(packed_ref, table_ref, payload_ref):
    groups = table_ref.shape[1] // LANES
    table = table_ref[...]
    low_half = lane((HIGH, LANES)) < LANES // 2
    for base in range(0, payload_ref.shape[0], HIGH):
        sides = []
        for side in range(2):
            packed = packed_ref[side, base : base + HIGH, :]
            wide = mm(one_hot_rows((packed & (HIGH - 1)).astype(f32)), table)
            low = packed >> 8
            picked = pick_group(wide, low >> 1, groups)
            sides.append(jnp.where((low & 1) == side, picked, swap_halves(picked)))
        payload_ref[base : base + HIGH, :] = jnp.where(low_half, sides[0], sides[1]).astype(bf16)


class Fetch:
    def __init__(self, sems, pairs):
        self.copies = [pltpu.make_async_copy(src, dst, sems.at[k]) for k, (src, dst) in enumerate(pairs)]
        for copy in self.copies:
            copy.start()

    def wait(self, *which):
        for k in which or range(len(self.copies)):
            self.copies[k].wait()


def row_chunks(ref):
    return [slice(base, base + PAIR) for base in range(0, ref.shape[0], PAIR)]


def first_kernel(
    layers,
    x_hbm,
    send_hbm,
    inner_hbm,
    outer_hbm,
    down_hbm,
    post_inner_hbm,
    post_outer_hbm,
    out_low_hbm,
    out_high_hbm,
    payload_ref,
    *rest,
):
    layer = 0
    split = [(w, n) for w in (post_inner_hbm, post_outer_hbm) for n in range(layers)]
    split += [(w, n) for w in (inner_hbm, outer_hbm) for n in range(1, layers)]
    split_out = rest[: len(split)]
    (
        x_ref,
        send_ref,
        inner_ref,
        outer_ref,
        down_ref,
        out_ref,
        table_ref,
        packed_ref,
        split_ref,
        sems,
        out_sems,
        load_sems,
        split_sems,
    ) = rest[len(split) :]
    rows_half = x_ref.shape[0] // 2
    fetch = Fetch(
        sems,
        [
            (send_hbm, send_ref),
            (inner_hbm.at[layer], inner_ref),
            (outer_hbm.at[layer], outer_ref),
            (down_hbm.at[layer], down_ref),
            (x_hbm.at[0:rows_half], x_ref.at[0:rows_half]),
            (x_hbm.at[rows_half : 2 * rows_half], x_ref.at[rows_half : 2 * rows_half]),
        ],
    )
    fetch.wait(0)
    pack_sends(send_ref, packed_ref)
    fetch.wait(1, 2, 3, 4)
    loads = Fetch(load_sems, [(w.at[n], split_ref.at[k]) for k, (w, n) in enumerate(split)])
    inner_half, outer_half, down_half = half_weight(inner_ref), half_weight(outer_ref), half_weight(down_ref)
    halves = [slice(0, rows_half), slice(rows_half, 2 * rows_half)]
    outs = [out_low_hbm, out_high_hbm]
    stores = [pltpu.make_async_copy(out_ref.at[h], outs[k], out_sems.at[k]) for k, h in enumerate(halves)]
    for k, c in enumerate(row_chunks(x_ref)):
        if c.start == rows_half:
            stores[0].start()
            fetch.wait(5)
            loads.wait()
            copies = Fetch(split_sems, [(split_ref.at[n], to) for n, to in enumerate(split_out)])
        rows = residual_rows(x_ref[c, :], inner_half, outer_half)
        out_ref[c, :] = rows
        table_ref[:, k * LANES : (k + 1) * LANES] = project_pair(rows, down_half)
    stores[1].start()
    write_payload(packed_ref, table_ref, payload_ref)
    for store in stores:
        store.wait()
    copies.wait()


def one_hot_columns(high_ref, slab, first, count, n):
    rows = [high_ref[slab, first + k : first + k + 1, :] for k in range(n // LANES)]
    high = jnp.concatenate(rows, axis=1).astype(f32)
    at = lax.broadcasted_iota(i32, (count, high.shape[1]), 0).astype(f32)
    return jnp.where(high == at, f32(1), f32(0)).astype(bf16)


def gather_messages(incoming_ref, return_low_ref, message_ref):
    slots = incoming_ref.shape[0]
    low_half = lane((slots, LANES)) < LANES // 2
    upper = jnp.where(low_half, 0, 1)
    groups = message_ref.shape[1] // LANES
    total = None
    parts = return_low_ref.shape[0] - 1
    for g in range(parts):
        m, side = divmod(g, 2)
        both = incoming_ref[:, m * LANES : (m + 1) * LANES].astype(f32)
        other = swap_halves(both)
        spread = jnp.where(low_half, both, other) if side == 0 else jnp.where(low_half, other, both)
        low = return_low_ref[g]
        piece = jnp.concatenate(
            [jnp.where(low == 2 * k + upper, spread, f32(0)).astype(bf16) for k in range(groups)], axis=1
        )
        part = mm(one_hot_columns(return_low_ref, parts, g * (slots // LANES), HIGH, slots), piece)
        total = part if total is None else total + part
    message_ref[...] = total.astype(bf16)


def join_rows(inner, message, up_half):
    zero = jnp.zeros_like(up_half)
    u = jnp.concatenate(
        [
            mm(message, jnp.concatenate([up_half, zero], axis=0)),
            mm(message, jnp.concatenate([zero, up_half], axis=0)),
        ],
        axis=0,
    )
    return ((inner.astype(f32) + silu_of_half(u)) * root_half).astype(bf16)


def middle_kernel(
    layer,
    incoming_ref,
    return_low_ref,
    x_low_ref,
    x_high_hbm,
    up_ref,
    post_inner_ref,
    post_outer_ref,
    send_ref,
    down_ref,
    inner_ref,
    outer_ref,
    out_hbm,
    payload_ref,
    x_high_ref,
    out_ref,
    message_ref,
    table_ref,
    packed_ref,
    sems,
    out_sems,
):
    rows_half = x_low_ref.shape[0]
    halves = [slice(0, rows_half), slice(rows_half, 2 * rows_half)]
    fetch = Fetch(sems, [(x_high_hbm, x_high_ref)])
    stores = [pltpu.make_async_copy(out_ref.at[h], out_hbm.at[h], out_sems.at[k]) for k, h in enumerate(halves)]
    gather_messages(incoming_ref, return_low_ref, message_ref)
    up_half = half_weight(up_ref.at[layer])
    post_inner_half, post_outer_half = half_weight(post_inner_ref), half_weight(post_outer_ref)
    inner_half, outer_half = half_weight(inner_ref), half_weight(outer_ref)
    down_half = half_weight(down_ref.at[layer + 1])
    for k, c in enumerate(row_chunks(out_ref)):
        if c.start == rows_half:
            stores[0].start()
            fetch.wait()
        half, base = divmod(c.start, rows_half)
        x = (x_low_ref, x_high_ref)[half][base : base + PAIR, :]
        joined = join_rows(x, message_ref[:, k * LANES : (k + 1) * LANES], up_half)
        state = residual_rows(joined, post_inner_half, post_outer_half)
        rows = residual_rows(state, inner_half, outer_half)
        out_ref[c, :] = rows
        table_ref[:, k * LANES : (k + 1) * LANES] = project_pair(rows, down_half)
    stores[1].start()
    pack_sends(send_ref, packed_ref)
    write_payload(packed_ref, table_ref, payload_ref)
    for store in stores:
        store.wait()


def last_kernel(
    layer,
    incoming_ref,
    return_low_ref,
    x_ref,
    up_ref,
    post_inner_ref,
    post_outer_ref,
    out_hbm,
    out_ref,
    message_ref,
    out_sems,
):
    gather_messages(incoming_ref, return_low_ref, message_ref)
    up_half = half_weight(up_ref.at[layer])
    post_inner_half, post_outer_half = half_weight(post_inner_ref), half_weight(post_outer_ref)
    chunks = row_chunks(x_ref)
    stores = []
    count = len(chunks)
    bounds = [0, count // 2, count - 1, count]
    for n in range(3):
        part = range(bounds[n], bounds[n + 1])
        for k in part:
            c = chunks[k]
            joined = join_rows(x_ref[c, :], message_ref[:, k * LANES : (k + 1) * LANES], up_half)
            out_ref[c, :] = residual_rows(joined, post_inner_half, post_outer_half)
        rows = slice(part[0] * PAIR, (part[-1] + 1) * PAIR)
        store = pltpu.make_async_copy(out_ref.at[rows], out_hbm.at[rows], out_sems.at[n])
        store.start()
        stores.append(store)
    for store in stores:
        store.wait()


def prepare_kernel(
    cap,
    cap_back,
    counts_ref,
    source_ref,
    target_ref,
    return_ref,
    basis_hbm,
    bilinear_hbm,
    basis_out,
    source_out,
    return_low_out,
    basis_ref,
    bilinear_ref,
    high_ref,
    sems,
):
    fetch = Fetch(sems, [(basis_hbm, basis_ref), (bilinear_hbm, bilinear_ref)])
    prepare_returns(cap_back, return_ref, return_low_out, high_ref)
    prepare_slots(cap, cap_back, counts_ref, source_ref, target_ref, source_out, basis_ref.shape)
    fetch.wait()
    turn_basis(basis_ref, basis_out)
    layers, trip, depth = bilinear_ref.shape
    width = basis_out.shape[2]
    slab = basis_out.shape[0] - 1
    for layer in range(layers):
        for piece in range(depth // width):
            base = (layer * (depth // width) + piece) * trip
            basis_out[slab, base : base + trip, :] = bilinear_ref[layer, :, piece * width : (piece + 1) * width]


def turn_basis(basis_ref, basis_out):
    blocks, width, span = basis_ref.shape
    sph = span // width
    groups = blocks // BLOCKS_IN_GROUP
    side_blocks = LANES // width
    to = lax.broadcasted_iota(i32, (span, span), 0)
    order = jnp.where(lane((span, span)) == (to % width) * sph + to // width, f32(1), f32(0)).astype(bf16)
    for g in range(groups):
        rows = jnp.concatenate(
            [
                basis_ref[g * side_blocks : (g + 1) * side_blocks].reshape(LANES, span),
                basis_ref[blocks // 2 + g * side_blocks : blocks // 2 + (g + 1) * side_blocks].reshape(LANES, span),
            ],
            axis=0,
        )
        basis_out[g] = mm_nt(order, rows).astype(bf16)


def spread_weight(basis_ref, layer, trip, weight_out):
    slab, _, width = basis_ref.shape
    slab -= 1
    depth = weight_out.shape[0] // 2
    zero = jnp.zeros((trip, LANES), bf16)
    for k in range(0, depth // trip, 2):
        piece, at = divmod(k * trip, width)
        base = (layer * (depth // width) + piece) * trip
        pair = jnp.transpose(basis_ref[slab, base : base + trip, at : at + LANES].astype(f32))
        both = jnp.concatenate([pair, pair], axis=1).astype(bf16)
        for j in range(2):
            w = both[j * trip : (j + 1) * trip]
            base = (k + j) * 2 * trip
            weight_out[base : base + trip, :] = jnp.concatenate([w, zero], axis=1)
            weight_out[base + trip : base + 2 * trip, :] = jnp.concatenate([zero, w], axis=1)


def prepare_slots(cap, cap_back, counts_ref, source_ref, target_ref, source_out, basis_shape):
    blocks, width, _ = basis_shape
    groups = blocks // BLOCKS_IN_GROUP
    chunks = source_ref.shape[1] // LANES
    half_cap = cap // 2
    for chunk in range(chunks):
        side, g = divmod(chunk, groups)
        cols = slice(chunk * LANES, (chunk + 1) * LANES)
        s = source_ref[:, cols]
        rho = (s // cap) * half_cap + s % half_cap
        half = (s // half_cap) % 2
        row = target_ref[:, cols]
        picks, codes, lows = columns_of(
            [rho & (HIGH - 1), (rho >> 8) * 2 + (half ^ side), (row % cap_back) // SLOT_ROWS]
        )
        rows = slice(side * LANES, (side + 1) * LANES)
        source_out[g, rows, :] = (picks + codes * HIGH).astype(i32) + lows.astype(i32) * (HIGH * HIGH)
        live = (lane(row.shape) + chunk * LANES) // width < counts_ref[0]
        high = jnp.where(live, (row // cap_back) * SLOT_ROWS + row % SLOT_ROWS, -1)
        source_out[groups, chunk : chunk + 1, :] = high


def prepare_returns(cap_back, return_ref, return_low_out, high_ref):
    parts = cap_back // SLOT_ROWS
    owners_in = LANES // cap_back
    for chunk in range(return_ref.shape[1] // LANES):
        row = return_ref[:, chunk * LANES : (chunk + 1) * LANES]
        high, low = columns_of([row & (HIGH - 1), row >> 8])
        low = low.astype(i32)
        for o in range(owners_in):
            for g in range(parts):
                to = slice((chunk * owners_in + o) * SLOT_ROWS, (chunk * owners_in + o + 1) * SLOT_ROWS)
                at = slice((o * parts + g) * SLOT_ROWS, (o * parts + g + 1) * SLOT_ROWS)
                return_low_out[g, to, :] = low[at]
                high_ref[g, to, :] = high[at]
    slots = return_low_out.shape[1]
    for g in range(parts):
        for chunk in range(slots // LANES):
            high = rows_of(high_ref[g, chunk * LANES : (chunk + 1) * LANES, :])
            at = g * (slots // LANES) + chunk
            return_low_out[parts, at : at + 1, :] = high[0:1, :].astype(i32)


def block_diagonal(kept, width):
    half_blocks = BLOCKS_IN_GROUP // 2
    zero = jnp.zeros((width, LANES), bf16)
    columns = []
    for j in range(half_blocks):
        pieces = []
        for side in range(2):
            for k in range(half_blocks):
                base = side * LANES + k * width
                pieces.append(kept[base : base + width] if k == j else zero)
        columns.append(jnp.concatenate(pieces, axis=0))
    return jnp.concatenate(columns, axis=1)


def owner_kernel(
    layer,
    arrived_ref,
    source_ref,
    basis_ref,
    out_ref,
    weight_ref,
    kept_ref,
    lhs_ref,
    spread_ref,
):
    slabs, span, group_rows = basis_ref.shape
    groups = slabs - 1
    spread_weight(basis_ref, layer, LANES // 2, weight_ref)
    half_blocks = BLOCKS_IN_GROUP // 2
    width = LANES // half_blocks
    sph = span // width
    tables = arrived_ref.shape[0] // HIGH
    table = jnp.concatenate([arrived_ref[m * HIGH : (m + 1) * HIGH, :] for m in range(tables)], axis=1)
    shape = (group_rows, LANES)
    own_half = (lax.broadcasted_iota(i32, shape, 0) >= LANES) == (lane(shape) >= LANES // 2)
    for g in range(groups):
        source = source_ref[g]
        wide = mm(one_hot_rows((source & (HIGH - 1)).astype(f32)), table)
        code = (source >> 8) & (HIGH - 1)
        picked = pick_group(wide, code >> 1, tables)
        turned = jnp.where((code & 1) == 1, swap_halves(picked), picked)
        kept_ref[g] = jnp.where(own_half, turned, f32(0)).astype(bf16)
    for g in range(groups):
        contracted = mm(basis_ref[g], block_diagonal(kept_ref[g], width)).astype(bf16)
        for j in range(half_blocks):
            rows = slice(g * LANES + j * width, g * LANES + (j + 1) * width)
            for k in range(sph):
                lhs_ref[rows, k * LANES : (k + 1) * LANES] = contracted[k * width : (k + 1) * width, j * LANES : (j + 1) * LANES]
    half_rows = lhs_ref.shape[0]
    chunk = min(half_rows, PAIR)
    upper = jnp.where(lane((chunk, LANES)) < LANES // 2, 0, 1)
    lane_groups = spread_ref.shape[1] // LANES
    for base in range(0, half_rows, chunk):
        partial = mm(lhs_ref[base : base + chunk, :], weight_ref[...])
        for side in range(2):
            rows = slice(side * half_rows + base, side * half_rows + base + chunk)
            at = slice(side * LANES, (side + 1) * LANES)
            first = base // LANES
            low = jnp.concatenate([source_ref[g, at, :] >> 16 for g in range(first, first + chunk // LANES)], axis=0)
            values = partial[:, at]
            for m in range(lane_groups):
                spread_ref[rows, m * LANES : (m + 1) * LANES] = jnp.where(low == 2 * m + upper, values, f32(0)).astype(bf16)
    total = None
    for base in range(0, spread_ref.shape[0], chunk):
        part = mm(one_hot_columns(source_ref, groups, base // LANES, out_ref.shape[0], chunk), spread_ref[base : base + chunk, :])
        total = part if total is None else total + part
    out_ref[...] = total.astype(bf16)


IN_HBM = pl.BlockSpec(memory_space=pl.ANY)
IN_VMEM = pl.BlockSpec(memory_space=pltpu.VMEM)
IN_SMEM = pl.BlockSpec(memory_space=pltpu.SMEM)


def run(kernel, name, in_specs, outs, scratch, operands, mib=32, flops=10**9):
    out_specs, out_shapes = zip(*outs)
    return pl.pallas_call(
        kernel,
        in_specs=in_specs,
        out_specs=list(out_specs),
        out_shape=list(out_shapes),
        scratch_shapes=scratch,
        compiler_params=pltpu.CompilerParams(vmem_limit_bytes=mib * MIB),
        cost_estimate=pl.CostEstimate(flops=flops, bytes_accessed=8 * 10**6, transcendentals=0),
        name=name,
    )(*operands)


def like(array):
    return pltpu.VMEM(array.shape, array.dtype)


def of_layer(array):
    return pltpu.VMEM(array.shape[1:], array.dtype)


def on_device(
    bond_states,
    block_counts,
    send_rows,
    source_slots,
    target_slots,
    return_rows,
    angular_basis,
    pre_inner,
    pre_outer,
    down_proj,
    bilinear,
    up_proj,
    post_inner,
    post_outer,
):
    axes = ("bond", "atom")
    peers = lax.axis_size("bond") * lax.axis_size("atom")
    rows, depth = bond_states.shape
    blocks, width, span = angular_basis.shape
    layers, _, trip = down_proj.shape
    cap = send_rows.shape[2]
    returns = return_rows.shape[1]
    cap_back = returns // peers
    lookup = peers * cap // 2
    slots = peers * SLOT_ROWS
    slot_lanes = cap_back // SLOT_ROWS * trip
    groups = blocks // BLOCKS_IN_GROUP
    group_rows = BLOCKS_IN_GROUP * width
    send = send_rows.reshape(peers, cap)
    down_t = jnp.swapaxes(down_proj, 1, 2)
    bilinear_t = jnp.swapaxes(bilinear, 1, 2)
    shape_of = jax.ShapeDtypeStruct
    row_shape = shape_of((rows, depth), bf16)
    payload_shape = shape_of((lookup, LANES), bf16)
    packed_scratch = pltpu.VMEM((2, lookup, LANES), i32)
    wide_scratch = pltpu.VMEM((HIGH, rows // HIGH * trip), bf16)
    row_scratch = pltpu.VMEM((rows, depth), bf16)

    def exchange(values, per_peer):
        values = values.reshape(peers, per_peer, values.shape[1])
        got = lax.all_to_all(values, axes, split_axis=0, concat_axis=0, tiled=True)
        return got.reshape(peers * per_peer, values.shape[2])

    weight_shape = shape_of((depth, depth), bf16)
    splits = 2 * layers + 2 * (layers - 1)
    half_shape = shape_of((rows // 2, depth), bf16)
    inner_low, inner_high, payload, *weights = run(
        functools.partial(first_kernel, layers),
        "first",
        [IN_HBM] * 7,
        [(IN_HBM, half_shape)] * 2 + [(IN_VMEM, payload_shape)] + [(IN_HBM, weight_shape)] * splits,
        [row_scratch, like(send), of_layer(pre_inner), of_layer(pre_outer), of_layer(down_t), row_scratch, wide_scratch]
        + [packed_scratch, pltpu.VMEM((splits, depth, depth), bf16)]
        + [pltpu.SemaphoreType.DMA((n,)) for n in (6, 2, splits, splits)],
        (bond_states, send, pre_inner, pre_outer, down_t, post_inner, post_outer),
        mib=60,
    )
    inner = (inner_low, inner_high)
    post_inners, post_outers = weights[:layers], weights[layers : 2 * layers]
    pre_inners = [None] + weights[2 * layers : 3 * layers - 1]
    pre_outers = [None] + weights[3 * layers - 1 :]

    parts = cap_back // SLOT_ROWS
    basis, source, return_low = run(
        functools.partial(prepare_kernel, cap, cap_back),
        "prepare",
        [IN_SMEM] + [IN_VMEM] * 3 + [IN_HBM] * 2,
        [
            (IN_VMEM, shape_of((groups + 1, span, group_rows), bf16)),
            (IN_VMEM, shape_of((groups + 1, group_rows, LANES), i32)),
            (IN_VMEM, shape_of((parts + 1, slots, LANES), i32)),
        ],
        [like(angular_basis), like(bilinear_t), pltpu.VMEM((parts, slots, LANES), f32), pltpu.SemaphoreType.DMA((2,))],
        (block_counts, source_slots, target_slots, return_rows, angular_basis, bilinear_t),
        flops=4 * 10**9,
    )

    out = None
    for layer in range(layers):
        arrived = exchange(payload, cap // 2)
        (slot_sums,) = run(
            functools.partial(owner_kernel, layer),
            "owner",
            [IN_VMEM] * 3,
            [(IN_VMEM, shape_of((slots, slot_lanes), bf16))],
            [
                pltpu.VMEM((bilinear.shape[1] * 2, 2 * LANES), bf16),
                pltpu.VMEM((groups, group_rows, LANES), bf16),
                pltpu.VMEM((blocks * width // 2, bilinear.shape[1] * 2), bf16),
                pltpu.VMEM((blocks * width, slot_lanes), bf16),
            ],
            (arrived, source, basis),
        )
        incoming = exchange(slot_sums, SLOT_ROWS)
        head = (incoming, return_low, *inner, up_proj, post_inners[layer], post_outers[layer])
        if layer + 1 < layers:
            rows_out, payload = run(
                functools.partial(middle_kernel, layer),
                "middle",
                [IN_VMEM] * 3 + [IN_HBM] + [IN_VMEM] * 7,
                [(IN_HBM, row_shape), (IN_VMEM, payload_shape)],
                [like(half_shape), row_scratch, wide_scratch, wide_scratch, packed_scratch]
                + [pltpu.SemaphoreType.DMA((1,)), pltpu.SemaphoreType.DMA((2,))],
                head + (send, down_t, pre_inners[layer + 1], pre_outers[layer + 1]),
                mib=49,
            )
            inner = (rows_out,)
        else:
            (out,) = run(
                functools.partial(last_kernel, layer),
                "last",
                [IN_VMEM] * 6,
                [(IN_HBM, row_shape)],
                [row_scratch, wide_scratch, pltpu.SemaphoreType.DMA((3,))],
                head,
            )
    return out


def solution(mesh):
    split = ("bond", "atom")
    in_specs = (
        P(split, None),
        P(split),
        P(split, None, None),
        P(split, None),
        P(split, None),
        P(split, None),
        P(split, None, None),
    ) + (P(),) * 7
    return jax.shard_map(on_device, mesh=mesh, in_specs=in_specs, out_specs=P(split, None), check_vma=False)
```

```python
import functools

import jax
import jax.numpy as jnp
from jax import lax
from jax.experimental import pallas as pl
from jax.experimental.pallas import tpu as pltpu
from jax.sharding import PartitionSpec as P

root_half = 0.7071067811865476
LANES = 128
HIGH = 256
PAIR = 512
BLOCKS_IN_GROUP = 8
SLOT_ROWS = 8
MIB = 1024 * 1024

bf16 = jnp.bfloat16
f32 = jnp.float32
i32 = jnp.int32


def mm(a, b):
    return jnp.dot(a, b, preferred_element_type=f32)


def mm_nt(a, b):
    return lax.dot_general(a, b, (((1,), (1,)), ((), ())), preferred_element_type=f32)


def silu_of_half(u):
    return u + u * jnp.tanh(u)


def half_weight(ref):
    return ref[...] * bf16(0.5)


def lane(shape):
    return lax.broadcasted_iota(i32, shape, 1)


def one_hot_rows(high):
    at = lane(high.shape).astype(f32)
    parts = [jnp.where(high == at + k * LANES, f32(1), f32(0)).astype(bf16) for k in range(HIGH // LANES)]
    return jnp.concatenate(parts, axis=1)


def on_diagonal(values):
    row = lax.broadcasted_iota(i32, values.shape, 0)
    return jnp.where(row == lane(values.shape), values, f32(0)).astype(bf16)


def columns_of(rows):
    ones = jnp.ones((LANES, LANES), bf16)
    stacked = jnp.concatenate([on_diagonal(jnp.broadcast_to(r.astype(f32), (LANES, LANES))) for r in rows], axis=0)
    wide = mm(stacked, ones)
    return [wide[k * LANES : (k + 1) * LANES] for k in range(len(rows))]


def rows_of(column):
    return mm(jnp.ones((LANES, LANES), bf16), on_diagonal(column))


def swap_halves(v):
    return pltpu.roll(v, v.shape[1] // 2, 1)


def pick_group(wide, group, count):
    picked = wide[:, :LANES]
    for m in range(1, count):
        picked = jnp.where(group == m, wide[:, m * LANES : (m + 1) * LANES], picked)
    return picked


def residual_rows(x, inner_half, outer_half):
    hidden = silu_of_half(mm(x, inner_half)).astype(bf16)
    return ((x.astype(f32) + silu_of_half(mm(hidden, outer_half))) * root_half).astype(bf16)


def project_pair(inner_rows, down_t):
    zero = jnp.zeros_like(down_t)
    left = jnp.concatenate([down_t, zero], axis=0)
    right = jnp.concatenate([zero, down_t], axis=0)
    u = mm_nt(inner_rows[:HIGH], left) + mm_nt(inner_rows[HIGH:], right)
    return silu_of_half(u).astype(bf16)


def pack_sends(send_ref, packed_ref):
    owners, cap = send_ref.shape
    half_cap = cap // 2
    pack = LANES // half_cap
    for base in range(0, owners, pack):
        packed = []
        for o in range(base, base + pack, LANES // cap):
            row = jnp.concatenate([send_ref[o + k : o + k + 1, :] for k in range(LANES // cap)], axis=1)
            high, low = columns_of([row & (HIGH - 1), row >> 8])
            packed.append((high + low * HIGH).astype(i32))
        packed = jnp.concatenate(packed, axis=0)
        rows = slice(base * half_cap, (base + pack) * half_cap)
        for side in range(2):
            at = [slice(k * cap + side * half_cap, k * cap + (side + 1) * half_cap) for k in range(pack)]
            packed_ref[side, rows, :] = jnp.concatenate([packed[t] for t in at], axis=0)


def write_payload(packed_ref, table_ref, payload_ref):
    groups = table_ref.shape[1] // LANES
    table = table_ref[...]
    low_half = lane((HIGH, LANES)) < LANES // 2
    for base in range(0, payload_ref.shape[0], HIGH):
        sides = []
        for side in range(2):
            packed = packed_ref[side, base : base + HIGH, :]
            wide = mm(one_hot_rows((packed & (HIGH - 1)).astype(f32)), table)
            low = packed >> 8
            picked = pick_group(wide, low >> 1, groups)
            sides.append(jnp.where((low & 1) == side, picked, swap_halves(picked)))
        payload_ref[base : base + HIGH, :] = jnp.where(low_half, sides[0], sides[1]).astype(bf16)


class Fetch:
    def __init__(self, sems, pairs):
        self.copies = [pltpu.make_async_copy(src, dst, sems.at[k]) for k, (src, dst) in enumerate(pairs)]
        for copy in self.copies:
            copy.start()

    def wait(self, *which):
        for k in which or range(len(self.copies)):
            self.copies[k].wait()


def row_chunks(ref):
    return [slice(base, base + PAIR) for base in range(0, ref.shape[0], PAIR)]


def first_kernel(
    layers,
    x_hbm,
    send_hbm,
    inner_hbm,
    outer_hbm,
    down_hbm,
    post_inner_hbm,
    post_outer_hbm,
    out_low_hbm,
    out_high_hbm,
    payload_ref,
    *rest,
):
    layer = 0
    split = [(w, n) for w in (post_inner_hbm, post_outer_hbm) for n in range(layers - 1)]
    split += [(w, n) for w in (inner_hbm, outer_hbm) for n in range(1, layers)]
    split_out = rest[: len(split)]
    (
        x_ref,
        send_ref,
        inner_ref,
        outer_ref,
        down_ref,
        out_ref,
        table_ref,
        packed_ref,
        split_ref,
        sems,
        out_sems,
        load_sems,
        split_sems,
    ) = rest[len(split) :]
    rows_half = x_ref.shape[0] // 2
    fetch = Fetch(
        sems,
        [
            (send_hbm, send_ref),
            (inner_hbm.at[layer], inner_ref),
            (outer_hbm.at[layer], outer_ref),
            (down_hbm.at[layer], down_ref),
            (x_hbm.at[0:rows_half], x_ref.at[0:rows_half]),
            (x_hbm.at[rows_half : 2 * rows_half], x_ref.at[rows_half : 2 * rows_half]),
        ],
    )
    fetch.wait(0)
    pack_sends(send_ref, packed_ref)
    fetch.wait(1, 2, 3, 4)
    loads = Fetch(load_sems, [(w.at[n], split_ref.at[k]) for k, (w, n) in enumerate(split)])
    inner_half, outer_half, down_half = half_weight(inner_ref), half_weight(outer_ref), half_weight(down_ref)
    halves = [slice(0, rows_half), slice(rows_half, 2 * rows_half)]
    outs = [out_low_hbm, out_high_hbm]
    stores = [pltpu.make_async_copy(out_ref.at[h], outs[k], out_sems.at[k]) for k, h in enumerate(halves)]
    for k, c in enumerate(row_chunks(x_ref)):
        if c.start == rows_half:
            stores[0].start()
            fetch.wait(5)
            loads.wait()
            copies = Fetch(split_sems, [(split_ref.at[n], to) for n, to in enumerate(split_out)])
        rows = residual_rows(x_ref[c, :], inner_half, outer_half)
        out_ref[c, :] = rows
        table_ref[:, k * LANES : (k + 1) * LANES] = project_pair(rows, down_half)
    stores[1].start()
    write_payload(packed_ref, table_ref, payload_ref)
    for store in stores:
        store.wait()
    copies.wait()


def one_hot_columns(high_ref, slab, first, count, n):
    rows = [high_ref[slab, first + k : first + k + 1, :] for k in range(n // LANES)]
    high = jnp.concatenate(rows, axis=1).astype(f32)
    at = lax.broadcasted_iota(i32, (count, high.shape[1]), 0).astype(f32)
    return jnp.where(high == at, f32(1), f32(0)).astype(bf16)


def gather_messages(incoming_ref, return_low_ref, message_ref):
    slots = incoming_ref.shape[0]
    low_half = lane((slots, LANES)) < LANES // 2
    upper = jnp.where(low_half, 0, 1)
    groups = message_ref.shape[1] // LANES
    total = None
    parts = return_low_ref.shape[0] - 1
    for g in range(parts):
        m, side = divmod(g, 2)
        both = incoming_ref[:, m * LANES : (m + 1) * LANES].astype(f32)
        other = swap_halves(both)
        spread = jnp.where(low_half, both, other) if side == 0 else jnp.where(low_half, other, both)
        low = return_low_ref[g]
        piece = jnp.concatenate(
            [jnp.where(low == 2 * k + upper, spread, f32(0)).astype(bf16) for k in range(groups)], axis=1
        )
        part = mm(one_hot_columns(return_low_ref, parts, g * (slots // LANES), HIGH, slots), piece)
        total = part if total is None else total + part
    message_ref[...] = total.astype(bf16)


def join_rows(inner, message, up_half):
    zero = jnp.zeros_like(up_half)
    u = jnp.concatenate(
        [
            mm(message, jnp.concatenate([up_half, zero], axis=0)),
            mm(message, jnp.concatenate([zero, up_half], axis=0)),
        ],
        axis=0,
    )
    return ((inner.astype(f32) + silu_of_half(u)) * root_half).astype(bf16)


def middle_kernel(
    layer,
    incoming_ref,
    return_low_ref,
    x_low_ref,
    x_high_hbm,
    up_ref,
    post_inner_ref,
    post_outer_ref,
    send_ref,
    down_ref,
    inner_ref,
    outer_ref,
    out_hbm,
    payload_ref,
    x_high_ref,
    out_ref,
    message_ref,
    table_ref,
    packed_ref,
    sems,
    out_sems,
):
    rows_half = x_low_ref.shape[0]
    halves = [slice(0, rows_half), slice(rows_half, 2 * rows_half)]
    fetch = Fetch(sems, [(x_high_hbm, x_high_ref)])
    stores = [pltpu.make_async_copy(out_ref.at[h], out_hbm.at[h], out_sems.at[k]) for k, h in enumerate(halves)]
    gather_messages(incoming_ref, return_low_ref, message_ref)
    up_half = half_weight(up_ref.at[layer])
    post_inner_half, post_outer_half = half_weight(post_inner_ref), half_weight(post_outer_ref)
    inner_half, outer_half = half_weight(inner_ref), half_weight(outer_ref)
    down_half = half_weight(down_ref.at[layer + 1])
    for k, c in enumerate(row_chunks(out_ref)):
        if c.start == rows_half:
            stores[0].start()
            fetch.wait()
        half, base = divmod(c.start, rows_half)
        x = (x_low_ref, x_high_ref)[half][base : base + PAIR, :]
        joined = join_rows(x, message_ref[:, k * LANES : (k + 1) * LANES], up_half)
        state = residual_rows(joined, post_inner_half, post_outer_half)
        rows = residual_rows(state, inner_half, outer_half)
        out_ref[c, :] = rows
        table_ref[:, k * LANES : (k + 1) * LANES] = project_pair(rows, down_half)
    stores[1].start()
    pack_sends(send_ref, packed_ref)
    write_payload(packed_ref, table_ref, payload_ref)
    for store in stores:
        store.wait()


def last_kernel(
    layer,
    incoming_ref,
    return_low_ref,
    x_ref,
    up_ref,
    post_inner_ref,
    post_outer_ref,
    out_hbm,
    out_ref,
    message_ref,
    out_sems,
):
    gather_messages(incoming_ref, return_low_ref, message_ref)
    up_half = half_weight(up_ref.at[layer])
    post_inner_half, post_outer_half = half_weight(post_inner_ref.at[layer]), half_weight(post_outer_ref.at[layer])
    chunks = row_chunks(x_ref)
    stores = []
    count = len(chunks)
    bounds = [0, count // 2, count - 1, count]
    for n in range(3):
        part = range(bounds[n], bounds[n + 1])
        for k in part:
            c = chunks[k]
            joined = join_rows(x_ref[c, :], message_ref[:, k * LANES : (k + 1) * LANES], up_half)
            out_ref[c, :] = residual_rows(joined, post_inner_half, post_outer_half)
        rows = slice(part[0] * PAIR, (part[-1] + 1) * PAIR)
        store = pltpu.make_async_copy(out_ref.at[rows], out_hbm.at[rows], out_sems.at[n])
        store.start()
        stores.append(store)
    for store in stores:
        store.wait()


def prepare_kernel(
    cap,
    cap_back,
    counts_ref,
    source_ref,
    target_ref,
    return_ref,
    basis_hbm,
    bilinear_hbm,
    basis_out,
    source_out,
    return_low_out,
    basis_ref,
    bilinear_ref,
    high_ref,
    sems,
):
    fetch = Fetch(sems, [(basis_hbm, basis_ref), (bilinear_hbm, bilinear_ref)])
    prepare_returns(cap_back, return_ref, return_low_out, high_ref)
    prepare_slots(cap, cap_back, counts_ref, source_ref, target_ref, source_out, basis_ref.shape)
    fetch.wait()
    turn_basis(basis_ref, basis_out)
    layers, trip, depth = bilinear_ref.shape
    width = basis_out.shape[2]
    slab = basis_out.shape[0] - 1
    for layer in range(layers):
        for piece in range(depth // width):
            base = (layer * (depth // width) + piece) * trip
            basis_out[slab, base : base + trip, :] = bilinear_ref[layer, :, piece * width : (piece + 1) * width]


def turn_basis(basis_ref, basis_out):
    blocks, width, span = basis_ref.shape
    sph = span // width
    groups = blocks // BLOCKS_IN_GROUP
    side_blocks = LANES // width
    to = lax.broadcasted_iota(i32, (span, span), 0)
    order = jnp.where(lane((span, span)) == (to % width) * sph + to // width, f32(1), f32(0)).astype(bf16)
    for g in range(groups):
        rows = jnp.concatenate(
            [
                basis_ref[g * side_blocks : (g + 1) * side_blocks].reshape(LANES, span),
                basis_ref[blocks // 2 + g * side_blocks : blocks // 2 + (g + 1) * side_blocks].reshape(LANES, span),
            ],
            axis=0,
        )
        basis_out[g] = mm_nt(order, rows).astype(bf16)


def spread_weight(basis_ref, layer, trip, weight_out):
    slab, _, width = basis_ref.shape
    slab -= 1
    depth = weight_out.shape[0] // 2
    zero = jnp.zeros((trip, LANES), bf16)
    for k in range(0, depth // trip, 2):
        piece, at = divmod(k * trip, width)
        base = (layer * (depth // width) + piece) * trip
        pair = jnp.transpose(basis_ref[slab, base : base + trip, at : at + LANES].astype(f32))
        both = jnp.concatenate([pair, pair], axis=1).astype(bf16)
        for j in range(2):
            w = both[j * trip : (j + 1) * trip]
            base = (k + j) * 2 * trip
            weight_out[base : base + trip, :] = jnp.concatenate([w, zero], axis=1)
            weight_out[base + trip : base + 2 * trip, :] = jnp.concatenate([zero, w], axis=1)


def prepare_slots(cap, cap_back, counts_ref, source_ref, target_ref, source_out, basis_shape):
    blocks, width, _ = basis_shape
    groups = blocks // BLOCKS_IN_GROUP
    chunks = source_ref.shape[1] // LANES
    half_cap = cap // 2
    for chunk in range(chunks):
        side, g = divmod(chunk, groups)
        cols = slice(chunk * LANES, (chunk + 1) * LANES)
        s = source_ref[:, cols]
        rho = (s // cap) * half_cap + s % half_cap
        half = (s // half_cap) % 2
        row = target_ref[:, cols]
        picks, codes, lows = columns_of(
            [rho & (HIGH - 1), (rho >> 8) * 2 + (half ^ side), (row % cap_back) // SLOT_ROWS]
        )
        rows = slice(side * LANES, (side + 1) * LANES)
        source_out[g, rows, :] = (picks + codes * HIGH).astype(i32) + lows.astype(i32) * (HIGH * HIGH)
        live = (lane(row.shape) + chunk * LANES) // width < counts_ref[0]
        high = jnp.where(live, (row // cap_back) * SLOT_ROWS + row % SLOT_ROWS, -1)
        source_out[groups, chunk : chunk + 1, :] = high


def prepare_returns(cap_back, return_ref, return_low_out, high_ref):
    parts = cap_back // SLOT_ROWS
    owners_in = LANES // cap_back
    for chunk in range(return_ref.shape[1] // LANES):
        row = return_ref[:, chunk * LANES : (chunk + 1) * LANES]
        high, low = columns_of([row & (HIGH - 1), row >> 8])
        low = low.astype(i32)
        for o in range(owners_in):
            for g in range(parts):
                to = slice((chunk * owners_in + o) * SLOT_ROWS, (chunk * owners_in + o + 1) * SLOT_ROWS)
                at = slice((o * parts + g) * SLOT_ROWS, (o * parts + g + 1) * SLOT_ROWS)
                return_low_out[g, to, :] = low[at]
                high_ref[g, to, :] = high[at]
    slots = return_low_out.shape[1]
    for g in range(parts):
        for chunk in range(slots // LANES):
            high = rows_of(high_ref[g, chunk * LANES : (chunk + 1) * LANES, :])
            at = g * (slots // LANES) + chunk
            return_low_out[parts, at : at + 1, :] = high[0:1, :].astype(i32)


def block_diagonal(kept, width):
    half_blocks = BLOCKS_IN_GROUP // 2
    zero = jnp.zeros((width, LANES), bf16)
    columns = []
    for j in range(half_blocks):
        pieces = []
        for side in range(2):
            for k in range(half_blocks):
                base = side * LANES + k * width
                pieces.append(kept[base : base + width] if k == j else zero)
        columns.append(jnp.concatenate(pieces, axis=0))
    return jnp.concatenate(columns, axis=1)


def owner_kernel(
    layer,
    arrived_ref,
    source_ref,
    basis_ref,
    out_ref,
    weight_ref,
    kept_ref,
    lhs_ref,
    spread_ref,
):
    slabs, span, group_rows = basis_ref.shape
    groups = slabs - 1
    spread_weight(basis_ref, layer, LANES // 2, weight_ref)
    half_blocks = BLOCKS_IN_GROUP // 2
    width = LANES // half_blocks
    sph = span // width
    tables = arrived_ref.shape[0] // HIGH
    table = jnp.concatenate([arrived_ref[m * HIGH : (m + 1) * HIGH, :] for m in range(tables)], axis=1)
    shape = (group_rows, LANES)
    own_half = (lax.broadcasted_iota(i32, shape, 0) >= LANES) == (lane(shape) >= LANES // 2)
    for g in range(groups):
        source = source_ref[g]
        wide = mm(one_hot_rows((source & (HIGH - 1)).astype(f32)), table)
        code = (source >> 8) & (HIGH - 1)
        picked = pick_group(wide, code >> 1, tables)
        turned = jnp.where((code & 1) == 1, swap_halves(picked), picked)
        kept_ref[g] = jnp.where(own_half, turned, f32(0)).astype(bf16)
    for g in range(groups):
        contracted = mm(basis_ref[g], block_diagonal(kept_ref[g], width)).astype(bf16)
        for j in range(half_blocks):
            rows = slice(g * LANES + j * width, g * LANES + (j + 1) * width)
            for k in range(sph):
                lhs_ref[rows, k * LANES : (k + 1) * LANES] = contracted[k * width : (k + 1) * width, j * LANES : (j + 1) * LANES]
    half_rows = lhs_ref.shape[0]
    chunk = min(half_rows, PAIR)
    upper = jnp.where(lane((chunk, LANES)) < LANES // 2, 0, 1)
    lane_groups = spread_ref.shape[1] // LANES
    for base in range(0, half_rows, chunk):
        partial = mm(lhs_ref[base : base + chunk, :], weight_ref[...])
        for side in range(2):
            rows = slice(side * half_rows + base, side * half_rows + base + chunk)
            at = slice(side * LANES, (side + 1) * LANES)
            first = base // LANES
            low = jnp.concatenate([source_ref[g, at, :] >> 16 for g in range(first, first + chunk // LANES)], axis=0)
            values = partial[:, at]
            for m in range(lane_groups):
                spread_ref[rows, m * LANES : (m + 1) * LANES] = jnp.where(low == 2 * m + upper, values, f32(0)).astype(bf16)
    total = None
    for base in range(0, spread_ref.shape[0], chunk):
        part = mm(one_hot_columns(source_ref, groups, base // LANES, out_ref.shape[0], chunk), spread_ref[base : base + chunk, :])
        total = part if total is None else total + part
    out_ref[...] = total.astype(bf16)


IN_HBM = pl.BlockSpec(memory_space=pl.ANY)
IN_VMEM = pl.BlockSpec(memory_space=pltpu.VMEM)
IN_SMEM = pl.BlockSpec(memory_space=pltpu.SMEM)


def run(kernel, name, in_specs, outs, scratch, operands, mib=32, flops=10**9):
    out_specs, out_shapes = zip(*outs)
    return pl.pallas_call(
        kernel,
        in_specs=in_specs,
        out_specs=list(out_specs),
        out_shape=list(out_shapes),
        scratch_shapes=scratch,
        compiler_params=pltpu.CompilerParams(vmem_limit_bytes=mib * MIB),
        cost_estimate=pl.CostEstimate(flops=flops, bytes_accessed=8 * 10**6, transcendentals=0),
        name=name,
    )(*operands)


def like(array):
    return pltpu.VMEM(array.shape, array.dtype)


def of_layer(array):
    return pltpu.VMEM(array.shape[1:], array.dtype)


def on_device(
    bond_states,
    block_counts,
    send_rows,
    source_slots,
    target_slots,
    return_rows,
    angular_basis,
    pre_inner,
    pre_outer,
    down_proj,
    bilinear,
    up_proj,
    post_inner,
    post_outer,
):
    axes = ("bond", "atom")
    peers = lax.axis_size("bond") * lax.axis_size("atom")
    rows, depth = bond_states.shape
    blocks, width, span = angular_basis.shape
    layers, _, trip = down_proj.shape
    cap = send_rows.shape[2]
    returns = return_rows.shape[1]
    cap_back = returns // peers
    lookup = peers * cap // 2
    slots = peers * SLOT_ROWS
    slot_lanes = cap_back // SLOT_ROWS * trip
    groups = blocks // BLOCKS_IN_GROUP
    group_rows = BLOCKS_IN_GROUP * width
    send = send_rows.reshape(peers, cap)
    down_t = jnp.swapaxes(down_proj, 1, 2)
    bilinear_t = jnp.swapaxes(bilinear, 1, 2)
    shape_of = jax.ShapeDtypeStruct
    row_shape = shape_of((rows, depth), bf16)
    payload_shape = shape_of((lookup, LANES), bf16)
    packed_scratch = pltpu.VMEM((2, lookup, LANES), i32)
    wide_scratch = pltpu.VMEM((HIGH, rows // HIGH * trip), bf16)
    row_scratch = pltpu.VMEM((rows, depth), bf16)

    def exchange(values, per_peer):
        values = values.reshape(peers, per_peer, values.shape[1])
        got = lax.all_to_all(values, axes, split_axis=0, concat_axis=0, tiled=True)
        return got.reshape(peers * per_peer, values.shape[2])

    weight_shape = shape_of((depth, depth), bf16)
    splits = 4 * (layers - 1)
    half_shape = shape_of((rows // 2, depth), bf16)
    inner_low, inner_high, payload, *weights = run(
        functools.partial(first_kernel, layers),
        "first",
        [IN_HBM] * 7,
        [(IN_HBM, half_shape)] * 2 + [(IN_VMEM, payload_shape)] + [(IN_HBM, weight_shape)] * splits,
        [row_scratch, like(send), of_layer(pre_inner), of_layer(pre_outer), of_layer(down_t), row_scratch, wide_scratch]
        + [packed_scratch, pltpu.VMEM((splits, depth, depth), bf16)]
        + [pltpu.SemaphoreType.DMA((n,)) for n in (6, 2, splits, splits)],
        (bond_states, send, pre_inner, pre_outer, down_t, post_inner, post_outer),
        mib=60,
    )
    inner = (inner_low, inner_high)
    later = layers - 1
    post_inners, post_outers = weights[:later] + [post_inner], weights[later : 2 * later] + [post_outer]
    pre_inners, pre_outers = [None] + weights[2 * later : 3 * later], [None] + weights[3 * later :]

    parts = cap_back // SLOT_ROWS
    basis, source, return_low = run(
        functools.partial(prepare_kernel, cap, cap_back),
        "prepare",
        [IN_SMEM] + [IN_VMEM] * 3 + [IN_HBM] * 2,
        [
            (IN_VMEM, shape_of((groups + 1, span, group_rows), bf16)),
            (IN_VMEM, shape_of((groups + 1, group_rows, LANES), i32)),
            (IN_VMEM, shape_of((parts + 1, slots, LANES), i32)),
        ],
        [like(angular_basis), like(bilinear_t), pltpu.VMEM((parts, slots, LANES), f32), pltpu.SemaphoreType.DMA((2,))],
        (block_counts, source_slots, target_slots, return_rows, angular_basis, bilinear_t),
        flops=4 * 10**9,
    )

    out = None
    for layer in range(layers):
        arrived = exchange(payload, cap // 2)
        (slot_sums,) = run(
            functools.partial(owner_kernel, layer),
            "owner",
            [IN_VMEM] * 3,
            [(IN_VMEM, shape_of((slots, slot_lanes), bf16))],
            [
                pltpu.VMEM((bilinear.shape[1] * 2, 2 * LANES), bf16),
                pltpu.VMEM((groups, group_rows, LANES), bf16),
                pltpu.VMEM((blocks * width // 2, bilinear.shape[1] * 2), bf16),
                pltpu.VMEM((blocks * width, slot_lanes), bf16),
            ],
            (arrived, source, basis),
        )
        incoming = exchange(slot_sums, SLOT_ROWS)
        head = (incoming, return_low, *inner, up_proj, post_inners[layer], post_outers[layer])
        if layer + 1 < layers:
            rows_out, payload = run(
                functools.partial(middle_kernel, layer),
                "middle",
                [IN_VMEM] * 3 + [IN_HBM] + [IN_VMEM] * 7,
                [(IN_HBM, row_shape), (IN_VMEM, payload_shape)],
                [like(half_shape), row_scratch, wide_scratch, wide_scratch, packed_scratch]
                + [pltpu.SemaphoreType.DMA((1,)), pltpu.SemaphoreType.DMA((2,))],
                head + (send, down_t, pre_inners[layer + 1], pre_outers[layer + 1]),
                mib=49,
            )
            inner = (rows_out,)
        else:
            (out,) = run(
                functools.partial(last_kernel, layer),
                "last",
                [IN_VMEM] * 6,
                [(IN_HBM, row_shape)],
                [row_scratch, wide_scratch, pltpu.SemaphoreType.DMA((3,))],
                head,
            )
    return out


def solution(mesh):
    split = ("bond", "atom")
    in_specs = (
        P(split, None),
        P(split),
        P(split, None, None),
        P(split, None),
        P(split, None),
        P(split, None),
        P(split, None, None),
    ) + (P(),) * 7
    return jax.shard_map(on_device, mesh=mesh, in_specs=in_specs, out_specs=P(split, None), check_vma=False)
```

```python
import functools

import jax
import jax.numpy as jnp
from jax import lax
from jax.experimental import pallas as pl
from jax.experimental.pallas import tpu as pltpu
from jax.sharding import PartitionSpec as P

root_half = 0.7071067811865476
LANES = 128
HIGH = 256
PAIR = 512
BLOCKS_IN_GROUP = 8
SLOT_ROWS = 8
MIB = 1024 * 1024

bf16 = jnp.bfloat16
f32 = jnp.float32
i32 = jnp.int32


def mm(a, b):
    return jnp.dot(a, b, preferred_element_type=f32)


def mm_nt(a, b):
    return lax.dot_general(a, b, (((1,), (1,)), ((), ())), preferred_element_type=f32)


def silu_of_half(u):
    return u + u * jnp.tanh(u)


def half_weight(ref):
    return ref[...] * bf16(0.5)


def lane(shape):
    return lax.broadcasted_iota(i32, shape, 1)


def one_hot_rows(high):
    at = lane(high.shape).astype(f32)
    parts = [jnp.where(high == at + k * LANES, f32(1), f32(0)).astype(bf16) for k in range(HIGH // LANES)]
    return jnp.concatenate(parts, axis=1)


def on_diagonal(values):
    row = lax.broadcasted_iota(i32, values.shape, 0)
    return jnp.where(row == lane(values.shape), values, f32(0)).astype(bf16)


def columns_of(rows):
    ones = jnp.ones((LANES, LANES), bf16)
    stacked = jnp.concatenate([on_diagonal(jnp.broadcast_to(r.astype(f32), (LANES, LANES))) for r in rows], axis=0)
    wide = mm(stacked, ones)
    return [wide[k * LANES : (k + 1) * LANES] for k in range(len(rows))]


def rows_of(column):
    return mm(jnp.ones((LANES, LANES), bf16), on_diagonal(column))


def swap_halves(v):
    return pltpu.roll(v, v.shape[1] // 2, 1)


def pick_group(wide, group, count):
    picked = wide[:, :LANES]
    for m in range(1, count):
        picked = jnp.where(group == m, wide[:, m * LANES : (m + 1) * LANES], picked)
    return picked


def residual_rows(x, inner_half, outer_half):
    hidden = silu_of_half(mm(x, inner_half)).astype(bf16)
    return ((x.astype(f32) + silu_of_half(mm(hidden, outer_half))) * root_half).astype(bf16)


def project_pair(inner_rows, down_t):
    zero = jnp.zeros_like(down_t)
    left = jnp.concatenate([down_t, zero], axis=0)
    right = jnp.concatenate([zero, down_t], axis=0)
    u = mm_nt(inner_rows[:HIGH], left) + mm_nt(inner_rows[HIGH:], right)
    return silu_of_half(u).astype(bf16)


def pack_sends(send_ref, packed_ref):
    owners, cap = send_ref.shape
    half_cap = cap // 2
    pack = LANES // half_cap
    for base in range(0, owners, pack):
        packed = []
        for o in range(base, base + pack, LANES // cap):
            row = jnp.concatenate([send_ref[o + k : o + k + 1, :] for k in range(LANES // cap)], axis=1)
            high, low = columns_of([row & (HIGH - 1), row >> 8])
            packed.append((high + low * HIGH).astype(i32))
        packed = jnp.concatenate(packed, axis=0)
        rows = slice(base * half_cap, (base + pack) * half_cap)
        for side in range(2):
            at = [slice(k * cap + side * half_cap, k * cap + (side + 1) * half_cap) for k in range(pack)]
            packed_ref[side, rows, :] = jnp.concatenate([packed[t] for t in at], axis=0)


def write_payload(packed_ref, table_ref, payload_ref):
    groups = table_ref.shape[1] // LANES
    table = table_ref[...]
    low_half = lane((HIGH, LANES)) < LANES // 2
    for base in range(0, payload_ref.shape[0], HIGH):
        sides = []
        for side in range(2):
            packed = packed_ref[side, base : base + HIGH, :]
            wide = mm(one_hot_rows((packed & (HIGH - 1)).astype(f32)), table)
            low = packed >> 8
            picked = pick_group(wide, low >> 1, groups)
            sides.append(jnp.where((low & 1) == side, picked, swap_halves(picked)))
        payload_ref[base : base + HIGH, :] = jnp.where(low_half, sides[0], sides[1]).astype(bf16)


class Fetch:
    def __init__(self, sems, pairs):
        self.copies = [pltpu.make_async_copy(src, dst, sems.at[k]) for k, (src, dst) in enumerate(pairs)]
        for copy in self.copies:
            copy.start()

    def wait(self, *which):
        for k in which or range(len(self.copies)):
            self.copies[k].wait()


def row_chunks(ref):
    return [slice(base, base + PAIR) for base in range(0, ref.shape[0], PAIR)]


def first_kernel(
    layers,
    x_hbm,
    send_hbm,
    inner_hbm,
    outer_hbm,
    down_hbm,
    post_inner_hbm,
    post_outer_hbm,
    out_low_hbm,
    out_high_hbm,
    payload_ref,
    *rest,
):
    layer = 0
    split = [(w, n) for w in (post_inner_hbm, post_outer_hbm) for n in range(layers - 1)]
    split += [(w, n) for w in (inner_hbm, outer_hbm) for n in range(1, layers)]
    split_out = rest[: len(split)]
    (
        x_ref,
        send_ref,
        inner_ref,
        outer_ref,
        down_ref,
        out_ref,
        table_ref,
        packed_ref,
        split_ref,
        sems,
        out_sems,
        load_sems,
        split_sems,
    ) = rest[len(split) :]
    rows_half = x_ref.shape[0] // 2
    fetch = Fetch(
        sems,
        [
            (send_hbm, send_ref),
            (inner_hbm.at[layer], inner_ref),
            (outer_hbm.at[layer], outer_ref),
            (down_hbm.at[layer], down_ref),
            (x_hbm.at[0:rows_half], x_ref.at[0:rows_half]),
            (x_hbm.at[rows_half : 2 * rows_half], x_ref.at[rows_half : 2 * rows_half]),
        ],
    )
    fetch.wait(0)
    pack_sends(send_ref, packed_ref)
    fetch.wait(1, 2, 3, 4)
    loads = Fetch(load_sems, [(w.at[n], split_ref.at[k]) for k, (w, n) in enumerate(split)])
    inner_half, outer_half, down_half = half_weight(inner_ref), half_weight(outer_ref), half_weight(down_ref)
    halves = [slice(0, rows_half), slice(rows_half, 2 * rows_half)]
    outs = [out_low_hbm, out_high_hbm]
    stores = [pltpu.make_async_copy(out_ref.at[h], outs[k], out_sems.at[k]) for k, h in enumerate(halves)]
    for k, c in enumerate(row_chunks(x_ref)):
        if c.start == rows_half:
            stores[0].start()
            fetch.wait(5)
            loads.wait()
            copies = Fetch(split_sems, [(split_ref.at[n], to) for n, to in enumerate(split_out)])
        rows = residual_rows(x_ref[c, :], inner_half, outer_half)
        out_ref[c, :] = rows
        table_ref[:, k * LANES : (k + 1) * LANES] = project_pair(rows, down_half)
    stores[1].start()
    write_payload(packed_ref, table_ref, payload_ref)
    for store in stores:
        store.wait()
    copies.wait()


def one_hot_columns(high_ref, slab, first, count, n):
    rows = [high_ref[slab, first + k : first + k + 1, :] for k in range(n // LANES)]
    high = jnp.concatenate(rows, axis=1).astype(f32)
    at = lax.broadcasted_iota(i32, (count, high.shape[1]), 0).astype(f32)
    return jnp.where(high == at, f32(1), f32(0)).astype(bf16)


def gather_messages(incoming_ref, return_low_ref, message_ref):
    slots = incoming_ref.shape[0]
    low_half = lane((slots, LANES)) < LANES // 2
    upper = jnp.where(low_half, 0, 1)
    groups = message_ref.shape[1] // LANES
    total = None
    parts = return_low_ref.shape[0] - 1
    for g in range(parts):
        m, side = divmod(g, 2)
        both = incoming_ref[:, m * LANES : (m + 1) * LANES].astype(f32)
        other = swap_halves(both)
        spread = jnp.where(low_half, both, other) if side == 0 else jnp.where(low_half, other, both)
        low = return_low_ref[g]
        piece = jnp.concatenate(
            [jnp.where(low == 2 * k + upper, spread, f32(0)).astype(bf16) for k in range(groups)], axis=1
        )
        part = mm(one_hot_columns(return_low_ref, parts, g * (slots // LANES), HIGH, slots), piece)
        total = part if total is None else total + part
    message_ref[...] = total.astype(bf16)


def join_rows(inner, message, up_half):
    zero = jnp.zeros_like(up_half)
    u = jnp.concatenate(
        [
            mm(message, jnp.concatenate([up_half, zero], axis=0)),
            mm(message, jnp.concatenate([zero, up_half], axis=0)),
        ],
        axis=0,
    )
    return ((inner.astype(f32) + silu_of_half(u)) * root_half).astype(bf16)


def middle_kernel(
    layer,
    incoming_ref,
    return_low_ref,
    x_low_ref,
    x_high_hbm,
    up_ref,
    post_inner_ref,
    post_outer_ref,
    send_ref,
    down_ref,
    inner_ref,
    outer_ref,
    out_hbm,
    payload_ref,
    x_high_ref,
    out_ref,
    message_ref,
    table_ref,
    packed_ref,
    sems,
    out_sems,
):
    rows_half = x_low_ref.shape[0]
    halves = [slice(0, rows_half), slice(rows_half, 2 * rows_half)]
    fetch = Fetch(sems, [(x_high_hbm, x_high_ref)])
    stores = [pltpu.make_async_copy(out_ref.at[h], out_hbm.at[h], out_sems.at[k]) for k, h in enumerate(halves)]
    gather_messages(incoming_ref, return_low_ref, message_ref)
    up_half = half_weight(up_ref.at[layer])
    post_inner_half, post_outer_half = half_weight(post_inner_ref), half_weight(post_outer_ref)
    inner_half, outer_half = half_weight(inner_ref), half_weight(outer_ref)
    down_half = half_weight(down_ref.at[layer + 1])
    for k, c in enumerate(row_chunks(out_ref)):
        if c.start == rows_half:
            stores[0].start()
            fetch.wait()
        half, base = divmod(c.start, rows_half)
        x = (x_low_ref, x_high_ref)[half][base : base + PAIR, :]
        joined = join_rows(x, message_ref[:, k * LANES : (k + 1) * LANES], up_half)
        state = residual_rows(joined, post_inner_half, post_outer_half)
        rows = residual_rows(state, inner_half, outer_half)
        out_ref[c, :] = rows
        table_ref[:, k * LANES : (k + 1) * LANES] = project_pair(rows, down_half)
    stores[1].start()
    pack_sends(send_ref, packed_ref)
    write_payload(packed_ref, table_ref, payload_ref)
    for store in stores:
        store.wait()


def last_kernel(
    layer,
    incoming_ref,
    return_low_ref,
    x_ref,
    up_ref,
    post_inner_ref,
    post_outer_ref,
    out_hbm,
    out_ref,
    message_ref,
    out_sems,
):
    gather_messages(incoming_ref, return_low_ref, message_ref)
    up_half = half_weight(up_ref.at[layer])
    post_inner_half, post_outer_half = half_weight(post_inner_ref.at[layer]), half_weight(post_outer_ref.at[layer])
    chunks = row_chunks(x_ref)
    stores = []
    count = len(chunks)
    bounds = [0, count // 2, count - 1, count]
    for n in range(3):
        part = range(bounds[n], bounds[n + 1])
        for k in part:
            c = chunks[k]
            joined = join_rows(x_ref[c, :], message_ref[:, k * LANES : (k + 1) * LANES], up_half)
            out_ref[c, :] = residual_rows(joined, post_inner_half, post_outer_half)
        rows = slice(part[0] * PAIR, (part[-1] + 1) * PAIR)
        store = pltpu.make_async_copy(out_ref.at[rows], out_hbm.at[rows], out_sems.at[n])
        store.start()
        stores.append(store)
    for store in stores:
        store.wait()


def prepare_kernel(
    cap,
    cap_back,
    counts_ref,
    source_ref,
    target_ref,
    return_ref,
    basis_hbm,
    bilinear_hbm,
    basis_out,
    source_out,
    return_low_out,
    basis_ref,
    bilinear_ref,
    high_ref,
    sems,
):
    fetch = Fetch(sems, [(basis_hbm, basis_ref), (bilinear_hbm, bilinear_ref)])
    prepare_returns(cap_back, return_ref, return_low_out, high_ref)
    prepare_slots(cap, cap_back, counts_ref, source_ref, target_ref, source_out, basis_ref.shape)
    fetch.wait()
    turn_basis(basis_ref, basis_out)
    layers, trip, depth = bilinear_ref.shape
    width = basis_out.shape[2]
    slab = basis_out.shape[0] - 1
    for layer in range(layers):
        for piece in range(depth // width):
            base = (layer * (depth // width) + piece) * trip
            basis_out[slab, base : base + trip, :] = bilinear_ref[layer, :, piece * width : (piece + 1) * width]


def turn_basis(basis_ref, basis_out):
    blocks, width, span = basis_ref.shape
    sph = span // width
    groups = blocks // BLOCKS_IN_GROUP
    side_blocks = LANES // width
    to = lax.broadcasted_iota(i32, (span, span), 0)
    order = jnp.where(lane((span, span)) == (to % width) * sph + to // width, f32(1), f32(0)).astype(bf16)
    for g in range(groups):
        rows = jnp.concatenate(
            [
                basis_ref[g * side_blocks : (g + 1) * side_blocks].reshape(LANES, span),
                basis_ref[blocks // 2 + g * side_blocks : blocks // 2 + (g + 1) * side_blocks].reshape(LANES, span),
            ],
            axis=0,
        )
        basis_out[g] = mm_nt(order, rows).astype(bf16)


def spread_weight(basis_ref, layer, trip, weight_out):
    slab, _, width = basis_ref.shape
    slab -= 1
    depth = weight_out.shape[0] // 2
    zero = jnp.zeros((trip, LANES), bf16)
    for k in range(0, depth // trip, 2):
        piece, at = divmod(k * trip, width)
        base = (layer * (depth // width) + piece) * trip
        pair = jnp.transpose(basis_ref[slab, base : base + trip, at : at + LANES].astype(f32))
        both = jnp.concatenate([pair, pair], axis=1).astype(bf16)
        for j in range(2):
            w = both[j * trip : (j + 1) * trip]
            base = (k + j) * 2 * trip
            weight_out[base : base + trip, :] = jnp.concatenate([w, zero], axis=1)
            weight_out[base + trip : base + 2 * trip, :] = jnp.concatenate([zero, w], axis=1)


def prepare_slots(cap, cap_back, counts_ref, source_ref, target_ref, source_out, basis_shape):
    blocks, width, _ = basis_shape
    groups = blocks // BLOCKS_IN_GROUP
    chunks = source_ref.shape[1] // LANES
    half_cap = cap // 2
    for chunk in range(chunks):
        side, g = divmod(chunk, groups)
        cols = slice(chunk * LANES, (chunk + 1) * LANES)
        s = source_ref[:, cols]
        rho = (s // cap) * half_cap + s % half_cap
        half = (s // half_cap) % 2
        row = target_ref[:, cols]
        picks, codes, lows = columns_of(
            [rho & (HIGH - 1), (rho >> 8) * 2 + (half ^ side), (row % cap_back) // SLOT_ROWS]
        )
        rows = slice(side * LANES, (side + 1) * LANES)
        source_out[g, rows, :] = (picks + codes * HIGH).astype(i32) + lows.astype(i32) * (HIGH * HIGH)
        live = (lane(row.shape) + chunk * LANES) // width < counts_ref[0]
        high = jnp.where(live, (row // cap_back) * SLOT_ROWS + row % SLOT_ROWS, -1)
        source_out[groups, chunk : chunk + 1, :] = high


def prepare_returns(cap_back, return_ref, return_low_out, high_ref):
    parts = cap_back // SLOT_ROWS
    owners_in = LANES // cap_back
    for chunk in range(return_ref.shape[1] // LANES):
        row = return_ref[:, chunk * LANES : (chunk + 1) * LANES]
        high, low = columns_of([row & (HIGH - 1), row >> 8])
        low = low.astype(i32)
        for o in range(owners_in):
            for g in range(parts):
                to = slice((chunk * owners_in + o) * SLOT_ROWS, (chunk * owners_in + o + 1) * SLOT_ROWS)
                at = slice((o * parts + g) * SLOT_ROWS, (o * parts + g + 1) * SLOT_ROWS)
                return_low_out[g, to, :] = low[at]
                high_ref[g, to, :] = high[at]
    slots = return_low_out.shape[1]
    for g in range(parts):
        for chunk in range(slots // LANES):
            high = rows_of(high_ref[g, chunk * LANES : (chunk + 1) * LANES, :])
            at = g * (slots // LANES) + chunk
            return_low_out[parts, at : at + 1, :] = high[0:1, :].astype(i32)


def block_diagonal(kept, width):
    half_blocks = BLOCKS_IN_GROUP // 2
    zero = jnp.zeros((width, LANES), bf16)
    columns = []
    for j in range(half_blocks):
        pieces = []
        for side in range(2):
            for k in range(half_blocks):
                base = side * LANES + k * width
                pieces.append(kept[base : base + width] if k == j else zero)
        columns.append(jnp.concatenate(pieces, axis=0))
    return jnp.concatenate(columns, axis=1)


def owner_kernel(
    layer,
    arrived_ref,
    source_ref,
    basis_ref,
    out_ref,
    weight_ref,
    kept_ref,
    lhs_ref,
    spread_ref,
    *own,
):
    if own:
        fetch = Fetch(own[2], [(arrived_ref, own[0])])
        arrived_ref = own[0]
    slabs, span, group_rows = basis_ref.shape
    groups = slabs - 1
    spread_weight(basis_ref, layer, LANES // 2, weight_ref)
    if own:
        for g in range(groups):
            own[1][g] = one_hot_rows((source_ref[g] & (HIGH - 1)).astype(f32))
        fetch.wait()
    half_blocks = BLOCKS_IN_GROUP // 2
    width = LANES // half_blocks
    sph = span // width
    tables = arrived_ref.shape[0] // HIGH
    table = jnp.concatenate([arrived_ref[m * HIGH : (m + 1) * HIGH, :] for m in range(tables)], axis=1)
    shape = (group_rows, LANES)
    own_half = (lax.broadcasted_iota(i32, shape, 0) >= LANES) == (lane(shape) >= LANES // 2)
    for g in range(groups):
        source = source_ref[g]
        pick = own[1][g] if own else one_hot_rows((source & (HIGH - 1)).astype(f32))
        wide = mm(pick, table)
        code = (source >> 8) & (HIGH - 1)
        picked = pick_group(wide, code >> 1, tables)
        turned = jnp.where((code & 1) == 1, swap_halves(picked), picked)
        kept_ref[g] = jnp.where(own_half, turned, f32(0)).astype(bf16)
    for g in range(groups):
        contracted = mm(basis_ref[g], block_diagonal(kept_ref[g], width)).astype(bf16)
        for j in range(half_blocks):
            rows = slice(g * LANES + j * width, g * LANES + (j + 1) * width)
            for k in range(sph):
                lhs_ref[rows, k * LANES : (k + 1) * LANES] = contracted[k * width : (k + 1) * width, j * LANES : (j + 1) * LANES]
    half_rows = lhs_ref.shape[0]
    chunk = min(half_rows, PAIR)
    upper = jnp.where(lane((chunk, LANES)) < LANES // 2, 0, 1)
    lane_groups = spread_ref.shape[1] // LANES
    for base in range(0, half_rows, chunk):
        partial = mm(lhs_ref[base : base + chunk, :], weight_ref[...])
        for side in range(2):
            rows = slice(side * half_rows + base, side * half_rows + base + chunk)
            at = slice(side * LANES, (side + 1) * LANES)
            first = base // LANES
            low = jnp.concatenate([source_ref[g, at, :] >> 16 for g in range(first, first + chunk // LANES)], axis=0)
            values = partial[:, at]
            for m in range(lane_groups):
                spread_ref[rows, m * LANES : (m + 1) * LANES] = jnp.where(low == 2 * m + upper, values, f32(0)).astype(bf16)
    total = None
    for base in range(0, spread_ref.shape[0], chunk):
        part = mm(one_hot_columns(source_ref, groups, base // LANES, out_ref.shape[0], chunk), spread_ref[base : base + chunk, :])
        total = part if total is None else total + part
    out_ref[...] = total.astype(bf16)


IN_HBM = pl.BlockSpec(memory_space=pl.ANY)
IN_VMEM = pl.BlockSpec(memory_space=pltpu.VMEM)
IN_SMEM = pl.BlockSpec(memory_space=pltpu.SMEM)


def run(kernel, name, in_specs, outs, scratch, operands, mib=32, flops=10**9):
    out_specs, out_shapes = zip(*outs)
    return pl.pallas_call(
        kernel,
        in_specs=in_specs,
        out_specs=list(out_specs),
        out_shape=list(out_shapes),
        scratch_shapes=scratch,
        compiler_params=pltpu.CompilerParams(vmem_limit_bytes=mib * MIB),
        cost_estimate=pl.CostEstimate(flops=flops, bytes_accessed=8 * 10**6, transcendentals=0),
        name=name,
    )(*operands)


def like(array):
    return pltpu.VMEM(array.shape, array.dtype)


def of_layer(array):
    return pltpu.VMEM(array.shape[1:], array.dtype)


def on_device(
    bond_states,
    block_counts,
    send_rows,
    source_slots,
    target_slots,
    return_rows,
    angular_basis,
    pre_inner,
    pre_outer,
    down_proj,
    bilinear,
    up_proj,
    post_inner,
    post_outer,
):
    axes = ("bond", "atom")
    peers = lax.axis_size("bond") * lax.axis_size("atom")
    rows, depth = bond_states.shape
    blocks, width, span = angular_basis.shape
    layers, _, trip = down_proj.shape
    cap = send_rows.shape[2]
    returns = return_rows.shape[1]
    cap_back = returns // peers
    lookup = peers * cap // 2
    slots = peers * SLOT_ROWS
    slot_lanes = cap_back // SLOT_ROWS * trip
    groups = blocks // BLOCKS_IN_GROUP
    group_rows = BLOCKS_IN_GROUP * width
    send = send_rows.reshape(peers, cap)
    down_t = jnp.swapaxes(down_proj, 1, 2)
    bilinear_t = jnp.swapaxes(bilinear, 1, 2)
    shape_of = jax.ShapeDtypeStruct
    row_shape = shape_of((rows, depth), bf16)
    payload_shape = shape_of((lookup, LANES), bf16)
    packed_scratch = pltpu.VMEM((2, lookup, LANES), i32)
    wide_scratch = pltpu.VMEM((HIGH, rows // HIGH * trip), bf16)
    row_scratch = pltpu.VMEM((rows, depth), bf16)

    def exchange(values, per_peer):
        values = values.reshape(peers, per_peer, values.shape[1])
        got = lax.all_to_all(values, axes, split_axis=0, concat_axis=0, tiled=True)
        return got.reshape(peers * per_peer, values.shape[2])

    weight_shape = shape_of((depth, depth), bf16)
    splits = 4 * (layers - 1)
    half_shape = shape_of((rows // 2, depth), bf16)
    inner_low, inner_high, payload, *weights = run(
        functools.partial(first_kernel, layers),
        "first",
        [IN_HBM] * 7,
        [(IN_HBM, half_shape)] * 2 + [(IN_VMEM, payload_shape)] + [(IN_HBM, weight_shape)] * splits,
        [row_scratch, like(send), of_layer(pre_inner), of_layer(pre_outer), of_layer(down_t), row_scratch, wide_scratch]
        + [packed_scratch, pltpu.VMEM((splits, depth, depth), bf16)]
        + [pltpu.SemaphoreType.DMA((n,)) for n in (6, 2, splits, splits)],
        (bond_states, send, pre_inner, pre_outer, down_t, post_inner, post_outer),
        mib=60,
    )
    inner = (inner_low, inner_high)
    later = layers - 1
    post_inners, post_outers = weights[:later] + [post_inner], weights[later : 2 * later] + [post_outer]
    pre_inners, pre_outers = [None] + weights[2 * later : 3 * later], [None] + weights[3 * later :]

    parts = cap_back // SLOT_ROWS
    basis, source, return_low = run(
        functools.partial(prepare_kernel, cap, cap_back),
        "prepare",
        [IN_SMEM] + [IN_VMEM] * 3 + [IN_HBM] * 2,
        [
            (IN_VMEM, shape_of((groups + 1, span, group_rows), bf16)),
            (IN_VMEM, shape_of((groups + 1, group_rows, LANES), i32)),
            (IN_VMEM, shape_of((parts + 1, slots, LANES), i32)),
        ],
        [like(angular_basis), like(bilinear_t), pltpu.VMEM((parts, slots, LANES), f32), pltpu.SemaphoreType.DMA((2,))],
        (block_counts, source_slots, target_slots, return_rows, angular_basis, bilinear_t),
        flops=4 * 10**9,
    )

    out = None
    for layer in range(layers):
        arrived = exchange(payload, cap // 2)
        (slot_sums,) = run(
            functools.partial(owner_kernel, layer),
            "owner",
            [IN_HBM if layer == 0 else IN_VMEM] + [IN_VMEM] * 2,
            [(IN_VMEM, shape_of((slots, slot_lanes), bf16))],
            [
                pltpu.VMEM((bilinear.shape[1] * 2, 2 * LANES), bf16),
                pltpu.VMEM((groups, group_rows, LANES), bf16),
                pltpu.VMEM((blocks * width // 2, bilinear.shape[1] * 2), bf16),
                pltpu.VMEM((blocks * width, slot_lanes), bf16),
            ]
            + ([like(arrived), pltpu.VMEM((groups, group_rows, HIGH), bf16)] if layer == 0 else [])
            + ([pltpu.SemaphoreType.DMA((1,))] if layer == 0 else []),
            (arrived, source, basis),
        )
        incoming = exchange(slot_sums, SLOT_ROWS)
        head = (incoming, return_low, *inner, up_proj, post_inners[layer], post_outers[layer])
        if layer + 1 < layers:
            rows_out, payload = run(
                functools.partial(middle_kernel, layer),
                "middle",
                [IN_VMEM] * 3 + [IN_HBM] + [IN_VMEM] * 7,
                [(IN_HBM, row_shape), (IN_VMEM, payload_shape)],
                [like(half_shape), row_scratch, wide_scratch, wide_scratch, packed_scratch]
                + [pltpu.SemaphoreType.DMA((1,)), pltpu.SemaphoreType.DMA((2,))],
                head + (send, down_t, pre_inners[layer + 1], pre_outers[layer + 1]),
                mib=49,
            )
            inner = (rows_out,)
        else:
            (out,) = run(
                functools.partial(last_kernel, layer),
                "last",
                [IN_VMEM] * 6,
                [(IN_HBM, row_shape)],
                [row_scratch, wide_scratch, pltpu.SemaphoreType.DMA((3,))],
                head,
            )
    return out


def solution(mesh):
    split = ("bond", "atom")
    in_specs = (
        P(split, None),
        P(split),
        P(split, None, None),
        P(split, None),
        P(split, None),
        P(split, None),
        P(split, None, None),
    ) + (P(),) * 7
    return jax.shard_map(on_device, mesh=mesh, in_specs=in_specs, out_specs=P(split, None), check_vma=False)
```
